512 devices in a mesh: shard: 64 (over x, z, core), grp: 8 (over y).
Axes of the slice: x: 4, y: 8, z: 8, core: 2. Of those that a mesh axis runs over, the one named last changes fastest.
Arguments:
- emb_table: bfloat16 [131072, 192], P('shard'), may hold values from -3 to 3
- touched: int32 [64, 8, 64, 64], P('shard', 'grp'), may hold values from -1 to 2047, as said below
- bag_slots: int32 [1024, 384, 4], P('shard', 'grp'), may hold values from -1 to 4095, as said below
- feat_of_slot: int32 [8, 48], P('grp'), may hold values from -1 to 255, as said below
- lcb_weight: bfloat16 [256, 256], replicated, may hold values from -0.375 to 0.375
- proj_weight: bfloat16 [256, 64], replicated, may hold values from -0.375 to 0.375
- fm_weight: bfloat16 [64, 192], replicated, may hold values from -0.0546875 to 0.0546875
- ln_gain: float32 [192], replicated, may hold values from 0.5 to 1.5
- cotangent: bfloat16 [1024, 256, 192], P(('shard', 'grp')), may hold values from -6 to 6
Outputs:
- interacted: bfloat16 [1024, 256, 192], P(('shard', 'grp'))
- table_grad: float32 [131072, 192], P(('shard', 'grp'))
- lcb_grad: float32 [256, 256], replicated
- proj_grad: float32 [256, 64], replicated
- fm_grad: float32 [64, 192], replicated
The draws below stay inside these ranges and needn't reach their ends.
Inputs may be any that keep to these rules, and one draw needn't show every extreme that they name: `touched`: for each device of the batch and each owner, a list of 64 slots: one or more distinct local rows, then -1 to the end of the list. In every draw one owner's list is full from every device of the batch. `bag_slots`: each entry is -1 or a slot o * 64 + k of the device's own lists (its block of samples and its group) whose row in touched is not -1. The bag of a slot that feat_of_slot marks -1 is all -1; the bag of a live slot has one entry or more, its -1 entries after the others. `feat_of_slot`: each feature of 0 to 255 is held by exactly one slot over all groups; in each group the live slots come first, then -1.
All inputs are finite; a program needn't handle non-finite values.
Results may differ from the reference program's by a relative error of at most 0.013.
Values may be sent and summed in bfloat16 or wider, within the bound.
A program may use at most 64 MiB of HBM per device.

```python
import jax
import jax.numpy as jnp
from jax import lax

D = 192
F = 256
RANK = 64
B_DEV = 16
ROWS_DEV = 2048
CAP = 64
BAG = 4
FG_MAX = 48
TOKENS = 1024
ROWS = 131072
N_SHARD = 64
N_GRP = 8


def group_sizes(key):
    heavy_group = jax.random.randint(jax.random.fold_in(key, 101), (), 0, N_GRP)
    group_rank = (jnp.arange(N_GRP, dtype=jnp.int32) - heavy_group) % N_GRP
    spare_count = F - FG_MAX
    base_count = spare_count // (N_GRP - 1)
    extra_count = spare_count - base_count * (N_GRP - 1)
    sizes_now = jnp.where(group_rank == 0, FG_MAX, base_count + (group_rank - 1 < extra_count).astype(jnp.int32))
    return sizes_now.astype(jnp.int32)


def list_counts(key):
    counts = jax.random.randint(jax.random.fold_in(key, 102), (N_SHARD, N_GRP, N_SHARD), 1, CAP + 1)
    full_owner = jax.random.randint(jax.random.fold_in(key, 103), (), 0, N_SHARD)
    owner_line = jnp.arange(N_SHARD, dtype=jnp.int32)[None, None, :]
    counts = jnp.where(owner_line == full_owner, CAP, counts)
    counts = counts.at[0, 0, N_SHARD - 1].set(CAP)
    counts = counts.at[N_SHARD - 1, N_GRP - 1, (full_owner + 1) % N_SHARD].set(1)
    return counts.astype(jnp.int32)


def draw_touched(key, part):
    counts = list_counts(key)
    key = jax.random.fold_in(key, 3)
    draw_shape = (N_SHARD, N_GRP, N_SHARD)
    start_row = jax.random.randint(jax.random.fold_in(key, 1), draw_shape, 0, ROWS_DEV)
    start_row = start_row.at[0, 0].set(ROWS_DEV - 1)
    stride = 2 * jax.random.randint(jax.random.fold_in(key, 2), draw_shape, 0, ROWS_DEV // 2) + 1
    slot_pos = jnp.arange(CAP, dtype=jnp.int32)
    row_ids = (start_row[..., None] + slot_pos * stride[..., None]) % ROWS_DEV
    return jnp.where(slot_pos < counts[..., None], row_ids, -1).astype(jnp.int32)


def draw_bag_slots(key, part):
    sizes_now = group_sizes(key)
    counts = list_counts(key)
    key = jax.random.fold_in(key, 5)
    draw_shape = (N_SHARD, B_DEV, N_GRP, FG_MAX, BAG)
    owner_pick = jax.random.randint(jax.random.fold_in(key, 1), draw_shape, 0, N_SHARD)
    raw_pick = jax.random.randint(jax.random.fold_in(key, 2), draw_shape, 0, 1 << 20)
    length = jax.random.randint(jax.random.fold_in(key, 3), (N_SHARD, B_DEV, N_GRP, FG_MAX, 1), 1, BAG + 1)
    shard_line = jnp.arange(N_SHARD, dtype=jnp.int32).reshape(-1, 1, 1, 1, 1)
    sample_line = jnp.arange(B_DEV, dtype=jnp.int32).reshape(1, -1, 1, 1, 1)
    group_line = jnp.arange(N_GRP, dtype=jnp.int32).reshape(1, 1, -1, 1, 1)
    slot_line = jnp.arange(FG_MAX, dtype=jnp.int32).reshape(1, 1, 1, -1, 1)
    bag_line = jnp.arange(BAG, dtype=jnp.int32).reshape(1, 1, 1, 1, -1)
    live_count = counts[shard_line, group_line, owner_pick]
    position = raw_pick % live_count
    first_entry = (shard_line == 0) & (sample_line == 0) & (group_line == 0) & (slot_line == 0) & (bag_line == 0)
    owner_pick = jnp.where(first_entry, N_SHARD - 1, owner_pick)
    position = jnp.where(first_entry, CAP - 1, position)
    slot_value = owner_pick * CAP + position
    is_live = (slot_line < sizes_now.reshape(1, 1, -1, 1, 1)) & (bag_line < length)
    result = jnp.where(is_live, slot_value, -1)
    return result.reshape(N_SHARD * B_DEV, N_GRP * FG_MAX, BAG).astype(jnp.int32)


def draw_feat_of_slot(key, part):
    sizes_now = group_sizes(key)
    key = jax.random.fold_in(key, 7)
    shuffled = jax.random.permutation(key, F).astype(jnp.int32)
    offsets = jnp.cumsum(sizes_now) - sizes_now
    slot_line = jnp.arange(FG_MAX, dtype=jnp.int32)
    flat_index = offsets[:, None] + slot_line[None, :]
    feature_ids = shuffled[jnp.minimum(flat_index, F - 1)]
    return jnp.where(slot_line[None, :] < sizes_now[:, None], feature_ids, -1).astype(jnp.int32)


def block_levels(key, extent, pieces, smallest, top_value):
    def one(dim, blocks):
        heights = jax.random.uniform(jax.random.fold_in(jax.random.fold_in(key, 6), dim), (blocks,), jnp.float32, smallest / len(pieces), top_value / len(pieces))
        return jnp.repeat(jnp.exp(heights), extent[dim] // blocks).reshape((-1,) + (1,) * (len(extent) - dim - 1))

    gain = one(*pieces[0])
    for cut in pieces[1:]:
        gain = gain * one(*cut)
    return gain


def gaussian(key, extent, width, limit, pieces=(), kind=jnp.bfloat16):
    gain = block_levels(key, extent, pieces, -0.22, 0.18) if pieces else 1.0
    entries = jax.random.normal(key, extent, jnp.float32) * width * gain
    return jnp.minimum(jnp.maximum(entries, -limit), limit).astype(kind)


def setup_inputs(seed: int = 0) -> dict:
    arg_keys = jax.random.split(jax.random.key(seed), 10)
    return {
        "emb_table": gaussian(arg_keys[0], (ROWS, D), 0.5, 3.0, ((0, 64),)),
        "touched": draw_touched(jax.random.fold_in(arg_keys[9], 71), 0),
        "bag_slots": draw_bag_slots(jax.random.fold_in(arg_keys[9], 71), 0),
        "feat_of_slot": draw_feat_of_slot(jax.random.fold_in(arg_keys[9], 71), 0),
        "lcb_weight": gaussian(arg_keys[4], (F, F), F ** -0.5, 0.375),
        "proj_weight": gaussian(arg_keys[5], (F, RANK), F ** -0.5, 0.375),
        "fm_weight": gaussian(arg_keys[6], (RANK, D), (RANK * D) ** -0.5, 0.0546875),
        "ln_gain": jnp.clip(1.0 + 0.1 * jax.random.normal(arg_keys[7], (D,), jnp.float32), 0.5, 1.5),
        "cotangent": gaussian(arg_keys[8], (TOKENS, F, D), 1.0, 6.0, ((0, 512),)),
    }


norm_epsilon = 1e-05

def layer_pass(embedded, lcb_weight, proj_weight, fm_weight, ln_gain, upstream):
    wide_x = embedded.astype(jnp.float32)
    mix_weight = lcb_weight.astype(jnp.float32)
    project = proj_weight.astype(jnp.float32)
    expand = fm_weight.astype(jnp.float32)
    linear_part = jnp.einsum('bfd,fg->bgd', wide_x, mix_weight)
    low_rank = lax.optimization_barrier(jnp.einsum('bfd,fr->bdr', wide_x, project).astype(jnp.bfloat16)).astype(jnp.float32)
    crossed = lax.optimization_barrier(jnp.einsum('bfd,bdr->bfr', wide_x, low_rank).astype(jnp.bfloat16)).astype(jnp.float32)
    fm_part = jnp.einsum('bfr,rd->bfd', crossed, expand)
    summed = wide_x + linear_part + fm_part
    center = summed - lax.optimization_barrier(jnp.mean(summed, axis=-1, keepdims=True))
    inv_std = lax.rsqrt(lax.optimization_barrier(jnp.mean(center * center, axis=-1, keepdims=True)) + norm_epsilon)
    normed = center * inv_std
    gain_row = ln_gain.astype(jnp.float32)
    result = (normed * gain_row).astype(jnp.bfloat16)
    scaled = upstream.astype(jnp.float32) * gain_row
    grad_sum = inv_std * (scaled - lax.optimization_barrier(jnp.mean(scaled, axis=-1, keepdims=True)) - normed * lax.optimization_barrier(jnp.mean(scaled * normed, axis=-1, keepdims=True)))
    grad_low = lax.optimization_barrier(grad_sum.astype(jnp.bfloat16)).astype(jnp.float32)
    grad_cross = lax.optimization_barrier(jnp.einsum('bfd,rd->bfr', grad_low, expand).astype(jnp.bfloat16)).astype(jnp.float32)
    fm_grad = jnp.einsum('bfr,bfd->rd', crossed, grad_low)
    grad_proj = lax.optimization_barrier(jnp.einsum('bfd,bfr->bdr', wide_x, grad_cross).astype(jnp.bfloat16)).astype(jnp.float32)
    proj_grad = jnp.einsum('bfd,bdr->fr', wide_x, grad_proj)
    lcb_grad = jnp.einsum('bfd,bgd->fg', wide_x, grad_low)
    grad_in = grad_sum + jnp.einsum('fg,bgd->bfd', mix_weight, grad_low) + jnp.einsum('bfr,bdr->bfd', grad_cross, low_rank) + jnp.einsum('fr,bdr->bfd', project, grad_proj)
    return (result, grad_in.astype(jnp.bfloat16), lcb_grad, proj_grad, fm_grad)

def reference(emb_table, touched, bag_slots, feat_of_slot, lcb_weight, proj_weight, fm_weight, ln_gain, cotangent):
    flat_feats = feat_of_slot.reshape(-1)
    slot_total = flat_feats.shape[0]
    target = jnp.where(flat_feats >= 0, flat_feats, F)
    slot_of_feature = jnp.zeros((F,), jnp.int32).at[target].set(jnp.arange(slot_total, dtype=jnp.int32), mode='drop')
    live_slot = (flat_feats >= 0)[None, :, None]
    safe_feats = jnp.maximum(flat_feats, 0)
    owner_base = (jnp.arange(N_SHARD, dtype=jnp.int32) * ROWS_DEV)[None, :, None]
    group_index = jnp.arange(N_GRP, dtype=jnp.int32)[None, :, None]
    bag_block = bag_slots.reshape(N_SHARD, B_DEV, N_GRP, FG_MAX, BAG)
    upstream_all = cotangent.reshape(N_SHARD, B_DEV, F, D)

    def block_step(running, inputs_now):
        table_acc, lcb_acc, proj_acc, fm_acc = running
        wanted, bags_now, upstream = inputs_now
        row_ids = (jnp.maximum(wanted, 0) + owner_base).reshape(N_GRP, N_SHARD * CAP)
        pooled = jnp.zeros((B_DEV, N_GRP, FG_MAX, D), jnp.float32)
        for bag_pos in range(BAG):
            bag_entry = bags_now[..., bag_pos]
            picked_rows = row_ids[group_index, jnp.maximum(bag_entry, 0)]
            pooled = pooled + jnp.where((bag_entry >= 0)[..., None], emb_table[picked_rows].astype(jnp.float32), 0.0)
        pooled = pooled.astype(jnp.bfloat16).reshape(B_DEV, N_GRP * FG_MAX, D)
        embedded = pooled[:, slot_of_feature, :]
        result, grad_in, lcb_part, proj_part, fm_part = layer_pass(embedded, lcb_weight, proj_weight, fm_weight, ln_gain, upstream)
        slot_grad_in = jnp.where(live_slot, grad_in[:, safe_feats, :], jnp.zeros((), jnp.bfloat16))
        slot_grad_in = slot_grad_in.reshape(B_DEV, N_GRP, FG_MAX, D).astype(jnp.float32)
        slot_grad = jnp.zeros((N_GRP, N_SHARD * CAP, D), jnp.float32)
        for bag_pos in range(BAG):
            bag_entry = bags_now[..., bag_pos]
            group_full = jnp.broadcast_to(group_index, bag_entry.shape)
            slot_grad = slot_grad.at[group_full, jnp.maximum(bag_entry, 0)].add(jnp.where((bag_entry >= 0)[..., None], slot_grad_in, 0.0))
        table_acc = table_acc.at[row_ids.reshape(-1)].add(slot_grad.reshape(-1, D))
        return ((table_acc, lcb_acc + lcb_part, proj_acc + proj_part, fm_acc + fm_part), result)
    start_state = (jnp.zeros((ROWS, D), jnp.float32), jnp.zeros((F, F), jnp.float32), jnp.zeros((F, RANK), jnp.float32), jnp.zeros((RANK, D), jnp.float32))
    final_state, outputs = lax.scan(block_step, start_state, (touched, bag_block, upstream_all))
    table_grad, lcb_grad, proj_grad, fm_grad = final_state
    interacted = outputs.reshape(TOKENS, F, D)
    return (interacted, table_grad, lcb_grad, proj_grad, fm_grad)
```

```python
import functools

import jax
import jax.numpy as jnp
from jax import lax
from jax.experimental import pallas as pl
from jax.experimental.pallas import tpu as pltpu
from jax.sharding import PartitionSpec as P

MESH = pl.DeviceIdType.MESH
norm_epsilon = 1e-05
LANES = 128
HALF = 64
BF = jnp.bfloat16
F32 = jnp.float32


def nn(a, b):
    return lax.dot_general(a, b, (((1,), (0,)), ((), ())), preferred_element_type=F32)


def nt(a, b):
    return lax.dot_general(a, b, (((1,), (1,)), ((), ())), preferred_element_type=F32)


def wait_all(ref, sem):
    pltpu.make_async_copy(ref, ref, sem).wait()


def pack_pair(x, low):
    m = x.shape[0] // 2
    turned = pltpu.roll(x, HALF, 1)
    even = jnp.where(low, x[:m], turned[m:])
    odd = jnp.where(low, turned[:m], x[m:])
    return even.astype(BF), odd.astype(BF)


def unpack_pair(even, odd, low):
    even, odd = even.astype(F32), odd.astype(F32)
    top = jnp.where(low, even, pltpu.roll(odd, HALF, 1))
    bottom = jnp.where(low, pltpu.roll(even, HALF, 1), odd)
    return jnp.concatenate([top, bottom], axis=0).astype(BF)


def kernel(
    X, Z, G,
    lists_ref, bag_ref, feat_ref, table_ref, lcb_ref, projt_ref, fm_ref, fmt_ref, gain_ref, cot_ref,
    inter_ref, tgrad_ref, lcbg_ref, projg_ref, fmg_ref,
    lists_in, feat_in, oh, mt, sbuf, rbuf, wide, pooled, esend, erecv, pm, gsend, grecv, gt,
    hsend, hrecv, tacc, jsend, jrecv, w, k1, a2, k2, b3, k3, c4, k4, d5, k5, total,
    send_sem, list_sem, row_sem, grad_sem, grp_sem,
):
    S = X * Z * 2
    groups = X * 2
    me_s = lax.axis_index("shard")
    me_g = lax.axis_index("grp")
    core = lax.rem(me_s, 2)
    me_z = lax.rem(lax.div(me_s, 2), Z)
    me_x = lax.div(me_s, 2 * Z)
    slot_rows = HALF * Z
    rows = table_ref.shape[1]
    width = table_ref.shape[0]
    features = lcb_ref.shape[0]
    bags = bag_ref.shape[0]
    bag_lanes = bag_ref.shape[1]

    def peer(q, back):
        i = lax.rem(q, Z)
        j = lax.div(q, Z)
        dc = lax.rem(j, 2)
        dx = lax.rem(lax.div(j, 2) + i, X)
        if back:
            x, z = lax.rem(me_x + X - dx, X), lax.rem(me_z + Z - i, Z)
        else:
            x, z = lax.rem(me_x + dx, X), lax.rem(me_z + i, Z)
        return (x * Z + z) * 2 + lax.rem(core + dc, 2)

    def send(src, dst, ssem, rsem, **where):
        pltpu.make_async_remote_copy(
            src_ref=src, dst_ref=dst, send_sem=ssem, recv_sem=rsem,
            device_id=where, device_id_type=MESH,
        ).start()

    def group_back(k):
        return lax.rem(me_g + G - k, G)

    def group_ahead(k):
        return lax.rem(me_g + k, G)

    barrier = pltpu.get_barrier_semaphore()

    def greet_shard(q, carry):
        pl.semaphore_signal(barrier, inc=1, device_id={"shard": peer(q, False)}, device_id_type=MESH)
        return carry

    def greet_group(k, carry):
        pl.semaphore_signal(barrier, inc=1, device_id={"grp": group_ahead(k)}, device_id_type=MESH)
        return carry

    lax.fori_loop(1, S, greet_shard, 0)
    lax.fori_loop(1, G, greet_group, 0)
    pl.semaphore_wait(barrier, S - 1 + G - 1)

    def send_list(q, carry):
        to = peer(q, True)
        send(lists_ref.at[to], lists_in.at[q], send_sem.at[0], list_sem.at[lax.div(q, Z)], shard=to)
        return carry

    lax.fori_loop(1, S, send_list, 0)
    lists_in[0] = lists_ref[me_s]

    def send_feat(k, carry):
        send(feat_ref, feat_in.at[k], send_sem.at[1], grp_sem.at[0], grp=group_back(k))
        return carry

    lax.fori_loop(1, G, send_feat, 0)
    feat_in[0] = feat_ref[...]

    low1 = lax.broadcasted_iota(jnp.int32, (1, LANES), 1) < HALF
    low = lax.broadcasted_iota(jnp.int32, (width // 2, LANES), 1) < HALF

    row_line = lax.broadcasted_iota(jnp.int32, (256, LANES), 0)

    def serve(j, first):
        if first:
            wait_all(lists_in.at[pl.ds(1, Z - 1)], list_sem.at[j])
        else:
            wait_all(lists_in.at[pl.ds(j * Z, Z)], list_sem.at[j])
        for p in range(Z // 2):
            want = jnp.where(low1, lists_in[j * Z + 2 * p], lists_in[j * Z + 2 * p + 1])
            for kb in range(rows // 256):
                hit = jnp.where(row_line == want - kb * 256, 1.0, 0.0).astype(BF)
                oh[j, kb * 256:(kb + 1) * 256, p * LANES:(p + 1) * LANES] = hit
        found = nn(table_ref[...], oh[j])
        for p in range(Z // 2):
            even, odd = pack_pair(found[:, p * LANES:(p + 1) * LANES], low)
            sbuf[j * Z + 2 * p] = even
            sbuf[j * Z + 2 * p + 1] = odd

        def send_rows(q, carry):
            send(sbuf.at[q], rbuf.at[q], send_sem.at[2], row_sem.at[j], shard=peer(q, False))
            return carry

        lax.fori_loop(j * Z + (1 if first else 0), j * Z + Z, send_rows, 0)

    serve(0, True)
    rbuf[0] = sbuf[0]

    def serve_step(j, carry):
        serve(j, False)
        return carry

    lax.fori_loop(1, groups, serve_step, 0)

    slot_line = lax.broadcasted_iota(jnp.int32, (HALF, LANES), 0)

    def count_step(j, carry):
        for i in range(Z):
            base = peer(j * Z + i, True) * HALF
            for c in range(bag_lanes // LANES):
                lanes = slice(c * LANES, (c + 1) * LANES)
                count = jnp.zeros((HALF, LANES), F32)
                for b in range(bags):
                    count = count + jnp.where(slot_line == bag_ref[b:b + 1, lanes] - base, 1.0, 0.0)
                mt[j, i * HALF:(i + 1) * HALF, lanes] = count.astype(BF)
        return carry

    lax.fori_loop(0, groups, count_step, 0)

    wait_all(feat_in.at[pl.ds(1, G - 1)], grp_sem.at[0])
    feat_line = lax.broadcasted_iota(jnp.int32, (features, LANES), 0)
    for k in range(G):
        held = feat_line == feat_in[k]
        pm[:features, k * LANES:(k + 1) * LANES] = jnp.where(held & low1, 1.0, 0.0).astype(BF)
        pm[features:, k * LANES:(k + 1) * LANES] = jnp.where(held & ~low1, 1.0, 0.0).astype(BF)

    pooled[...] = jnp.zeros_like(pooled)

    def pool(j, first):
        if first:
            wait_all(rbuf.at[pl.ds(1, Z - 1)], row_sem.at[j])
        else:
            wait_all(rbuf.at[pl.ds(j * Z, Z)], row_sem.at[j])
        for p in range(Z // 2):
            wide[:, p * LANES:(p + 1) * LANES] = unpack_pair(
                rbuf[j * Z + 2 * p], rbuf[j * Z + 2 * p + 1], low
            )
        pooled[...] += nn(wide[...], mt[j])

    pool(0, True)

    def pool_step(j, carry):
        pool(j, False)
        return carry

    lax.fori_loop(1, groups, pool_step, 0)

    for g in range(G):
        k = group_back(g)
        esend[k] = pooled[:, g * LANES:(g + 1) * LANES].astype(BF)

    def send_pooled(k, carry):
        send(esend.at[k], erecv.at[k], send_sem.at[3], grp_sem.at[1], grp=group_back(k))
        return carry

    lax.fori_loop(1, G, send_pooled, 0)
    erecv[0] = esend[0]
    wait_all(erecv.at[pl.ds(1, G - 1)], grp_sem.at[1])

    arrived = jnp.concatenate([erecv[k] for k in range(G)], axis=1)
    both = nt(arrived, pm[...]).astype(BF)
    lcb = lcb_ref[...]
    projt = projt_ref[...]
    fm = fm_ref[...]
    fmt = fmt_ref[...]
    gain = gain_ref[...]
    lcb_grad = jnp.zeros((features, features), F32)
    proj_grad = jnp.zeros(projt.shape, F32)
    fm_grad = jnp.zeros(fm.shape, F32)
    grads_in = []
    for n in range(2):
        xt = both[:, n * features:(n + 1) * features]
        x = nt(pm[n * features:(n + 1) * features, :], arrived).astype(BF)
        low_rank = nt(xt, projt).astype(BF)
        low_rank_t = nt(projt, xt).astype(BF)
        crossed_t = nn(low_rank_t, xt).astype(BF)
        summed = xt.astype(F32) + nn(xt, lcb) + nn(fmt, crossed_t)
        center = summed - jnp.mean(summed, axis=0, keepdims=True)
        inv_std = lax.rsqrt(jnp.mean(center * center, axis=0, keepdims=True) + norm_epsilon)
        normed = center * inv_std
        inter_ref[n] = (normed * gain).astype(BF)
        scaled = cot_ref[n].astype(F32) * gain
        grad_sum = inv_std * (
            scaled
            - jnp.mean(scaled, axis=0, keepdims=True)
            - normed * jnp.mean(scaled * normed, axis=0, keepdims=True)
        )
        grad_low = grad_sum.astype(BF)
        grad_cross_t = nn(fm, grad_low).astype(BF)
        grad_proj = nt(xt, grad_cross_t).astype(BF)
        grad_proj_t = nt(grad_cross_t, xt).astype(BF)
        fm_grad = fm_grad + nt(crossed_t, grad_low)
        proj_grad = proj_grad + nn(grad_proj_t, xt)
        lcb_grad = lcb_grad + nn(x, grad_low)
        grads_in.append((
            grad_sum + nt(grad_low, lcb) + nn(low_rank, grad_cross_t) + nn(grad_proj, projt)
        ).astype(BF))

    back = nn(jnp.concatenate(grads_in, axis=1), pm[...]).astype(BF)
    for k in range(G):
        gsend[k] = back[:, k * LANES:(k + 1) * LANES]

    def send_back(k, carry):
        send(gsend.at[k], grecv.at[k], send_sem.at[4], grp_sem.at[2], grp=group_ahead(k))
        return carry

    lax.fori_loop(1, G, send_back, 0)
    grecv[0] = gsend[0]

    chunk = w.shape[1] // Z
    flat = w.shape[0] * w.shape[1]
    total[...] = jnp.zeros_like(total)
    total[:features] = lcb_grad
    total[features:features + HALF] = proj_grad
    total[features + HALF:features + 2 * HALF, :width] = fm_grad
    for g in range(G):
        w[g] = total[g * Z * chunk:(g + 1) * Z * chunk]

    def send_w(k, carry):
        to = group_back(k)
        send(w.at[to], k1.at[k], send_sem.at[5], grp_sem.at[3], grp=to)
        return carry

    lax.fori_loop(1, G, send_w, 0)

    wait_all(grecv.at[pl.ds(1, G - 1)], grp_sem.at[2])
    for g in range(G):
        gt[:, g * LANES:(g + 1) * LANES] = grecv[group_back(g)]

    def give(j, first):
        slot_grad = nt(gt[...], mt[j])
        for p in range(Z // 2):
            even, odd = pack_pair(slot_grad[:, p * LANES:(p + 1) * LANES], low)
            hsend[j * Z + 2 * p] = even
            hsend[j * Z + 2 * p + 1] = odd

        def send_grads(q, carry):
            send(hsend.at[q], hrecv.at[q], send_sem.at[6], grad_sem.at[j], shard=peer(q, True))
            return carry

        lax.fori_loop(j * Z + (1 if first else 0), j * Z + Z, send_grads, 0)

    give(0, True)
    hrecv[0] = hsend[0]

    def give_step(j, carry):
        give(j, False)
        return carry

    lax.fori_loop(1, groups, give_step, 0)

    def shard_of(x, z, c):
        return (x * Z + z) * 2 + c

    wait_all(k1.at[pl.ds(1, G - 1)], grp_sem.at[3])
    part = w[me_g]
    for k in range(1, G):
        part = part + k1[k]
    for z in range(Z):
        a2[z] = part[z * chunk:(z + 1) * chunk]

    def send_z(k, carry):
        z = lax.rem(me_z + Z - k, Z)
        send(a2.at[z], k2.at[k], send_sem.at[7], grp_sem.at[4], shard=shard_of(me_x, z, core))
        return carry

    lax.fori_loop(1, Z, send_z, 0)
    wait_all(k2.at[pl.ds(1, Z - 1)], grp_sem.at[4])
    part = a2[me_z]
    for k in range(1, Z):
        part = part + k2[k]
    b3[...] = part
    k3[0] = part
    me_xc = me_x * 2 + core
    XC = X * 2

    def send_xc(k, carry):
        xc = lax.rem(me_xc + XC - k, XC)
        send(b3, k3.at[k], send_sem.at[8], grp_sem.at[5],
             shard=shard_of(lax.div(xc, 2), me_z, lax.rem(xc, 2)))
        return carry

    lax.fori_loop(1, XC, send_xc, 0)
    wait_all(k3.at[pl.ds(1, XC - 1)], grp_sem.at[5])
    part = k3[lax.rem(XC - me_xc, XC)]
    for s in range(1, XC):
        part = part + k3[lax.rem(s + XC - me_xc, XC)]
    c4[...] = part
    k4[0] = part

    def send_z_back(k, carry):
        z = lax.rem(me_z + Z - k, Z)
        send(c4, k4.at[k], send_sem.at[9], grp_sem.at[6], shard=shard_of(me_x, z, core))
        return carry

    lax.fori_loop(1, Z, send_z_back, 0)
    wait_all(k4.at[pl.ds(1, Z - 1)], grp_sem.at[6])
    for z in range(Z):
        d5[z * chunk:(z + 1) * chunk] = k4[lax.rem(z + Z - me_z, Z)]
    k5[0] = d5[...]

    def send_g_back(k, carry):
        send(d5, k5.at[k], send_sem.at[10], grp_sem.at[7], grp=group_back(k))
        return carry

    lax.fori_loop(1, G, send_g_back, 0)

    tacc[...] = jnp.zeros_like(tacc)

    def take(j, first):
        if first:
            wait_all(hrecv.at[pl.ds(1, Z - 1)], grad_sem.at[j])
        else:
            wait_all(hrecv.at[pl.ds(j * Z, Z)], grad_sem.at[j])
        for p in range(Z // 2):
            wide[:, p * LANES:(p + 1) * LANES] = unpack_pair(
                hrecv[j * Z + 2 * p], hrecv[j * Z + 2 * p + 1], low
            )
        per = rows // G
        for g in range(G):
            tacc[g] += nt(wide[...], oh[j, g * per:(g + 1) * per, :])

    take(0, True)

    def take_step(j, carry):
        take(j, False)
        return carry

    lax.fori_loop(1, groups, take_step, 0)

    def send_table(k, carry):
        to = group_back(k)
        jsend[k] = tacc[to].astype(BF)
        send(jsend.at[k], jrecv.at[k], send_sem.at[11], grp_sem.at[8], grp=to)
        return carry

    lax.fori_loop(1, G, send_table, 0)

    wait_all(k5.at[pl.ds(1, G - 1)], grp_sem.at[7])
    span = Z * chunk
    for g in range(G):
        total[g * span:(g + 1) * span] = k5[lax.rem(g + G - me_g, G)]
    lcbg_ref[...] = total[:features]
    projg_ref[...] = total[features:features + HALF]
    fmg_ref[...] = total[features + HALF:features + 2 * HALF, :width]

    wait_all(jrecv.at[pl.ds(1, G - 1)], grp_sem.at[8])
    out = tacc[me_g]
    for k in range(1, G):
        out = out + jrecv[k].astype(F32)
    tgrad_ref[...] = out

    wait_all(lists_in.at[pl.ds(1, S - 1)], send_sem.at[0])
    wait_all(feat_in.at[pl.ds(1, G - 1)], send_sem.at[1])
    wait_all(sbuf.at[pl.ds(1, S - 1)], send_sem.at[2])
    wait_all(esend.at[pl.ds(1, G - 1)], send_sem.at[3])
    wait_all(gsend.at[pl.ds(1, G - 1)], send_sem.at[4])
    wait_all(k1.at[pl.ds(1, G - 1)], send_sem.at[5])
    wait_all(hsend.at[pl.ds(1, S - 1)], send_sem.at[6])
    wait_all(k2.at[pl.ds(1, Z - 1)], send_sem.at[7])
    wait_all(k3.at[pl.ds(1, XC - 1)], send_sem.at[8])
    wait_all(k4.at[pl.ds(1, Z - 1)], send_sem.at[9])
    wait_all(k5.at[pl.ds(1, G - 1)], send_sem.at[10])
    wait_all(jsend.at[pl.ds(1, G - 1)], send_sem.at[11])


def shards(X, Z, emb_table, touched, bag_slots, feat_of_slot, lcb_weight, proj_weight, fm_weight,
           ln_gain, cotangent):
    G = lax.axis_size("grp")
    S = X * Z * 2
    wanted = touched[0, 0]
    lists = jnp.concatenate([wanted, wanted], axis=1).reshape(S, 1, LANES)
    samples, slots, bags = bag_slots.shape
    bag = jnp.pad(jnp.transpose(bag_slots, (2, 0, 1)), ((0, 0), (0, 0), (0, HALF - slots)),
                  constant_values=-1).reshape(bags, samples * HALF)
    feat = jnp.pad(feat_of_slot, ((0, 0), (0, HALF - slots)), constant_values=-1)
    feat = jnp.concatenate([feat, feat], axis=1)
    table_t = emb_table.T
    width, rows = table_t.shape
    features = lcb_weight.shape[0]
    rank = proj_weight.shape[1]
    groups = X * 2
    chunk = -(-(features + 2 * HALF) // (G * Z * 8)) * 8
    vm = pltpu.VMEM
    dma = pltpu.SemaphoreType.DMA
    fold = (width // 2, LANES)
    scratch = [
        vm((S, 1, LANES), jnp.int32),
        vm((G, 1, LANES), jnp.int32),
        vm((groups, rows, Z * HALF), BF),
        vm((groups, Z * HALF, samples * HALF), BF),
        vm((S,) + fold, BF),
        vm((S,) + fold, BF),
        vm((width, Z * HALF), BF),
        vm((width, samples * HALF), F32),
        vm((G, width, LANES), BF),
        vm((G, width, LANES), BF),
        vm((2 * features, G * LANES), BF),
        vm((G, width, LANES), BF),
        vm((G, width, LANES), BF),
        vm((width, samples * HALF), BF),
        vm((S,) + fold, BF),
        vm((S,) + fold, BF),
        vm((G, width, rows // G), F32),
        vm((G, width, rows // G), BF),
        vm((G, width, rows // G), BF),
        vm((G, Z * chunk, features), F32),
        vm((G, Z * chunk, features), F32),
        vm((Z, chunk, features), F32),
        vm((Z, chunk, features), F32),
        vm((chunk, features), F32),
        vm((X * 2, chunk, features), F32),
        vm((chunk, features), F32),
        vm((Z, chunk, features), F32),
        vm((Z * chunk, features), F32),
        vm((G, Z * chunk, features), F32),
        vm((G * Z * chunk, features), F32),
        dma((12,)),
        dma((groups,)),
        dma((groups,)),
        dma((groups,)),
        dma((9,)),
    ]
    whole = pl.BlockSpec(memory_space=pltpu.VMEM)
    inter, tgrad, lcbg, projg, fmg = pl.pallas_call(
        functools.partial(kernel, X, Z, G),
        out_shape=(
            jax.ShapeDtypeStruct((2, width, features), BF),
            jax.ShapeDtypeStruct((width, rows // G), F32),
            jax.ShapeDtypeStruct((features, features), F32),
            jax.ShapeDtypeStruct((rank, features), F32),
            jax.ShapeDtypeStruct((rank, width), F32),
        ),
        in_specs=[whole] * 10,
        out_specs=[whole] * 5,
        scratch_shapes=scratch,
        compiler_params=pltpu.CompilerParams(
            collective_id=0, has_side_effects=True, vmem_limit_bytes=58 * 1024 * 1024
        ),
    )(
        lists, bag, feat, table_t, lcb_weight, proj_weight.T, fm_weight, fm_weight.T,
        ln_gain.reshape(-1, 1), jnp.transpose(cotangent, (0, 2, 1)),
    )
    return (jnp.transpose(inter, (0, 2, 1)), tgrad.T, lcbg, projg.T, fmg)


def solution(mesh):
    S = mesh.shape["shard"]
    Z = mesh.shape["grp"]
    X = S // (2 * Z)
    placed = (
        P("shard", None),
        P("shard", "grp", None, None),
        P("shard", "grp", None),
        P("grp", None),
        P(),
        P(),
        P(),
        P(),
        P(("shard", "grp"), None, None),
    )
    return jax.shard_map(
        functools.partial(shards, X, Z),
        mesh=mesh,
        in_specs=placed,
        out_specs=(P(("shard", "grp"), None, None), P(("shard", "grp"), None), P(), P(), P()),
        check_vma=False,
    )
```

```python
import functools

import jax
import jax.numpy as jnp
from jax import lax
from jax.experimental import pallas as pl
from jax.experimental.pallas import tpu as pltpu
from jax.sharding import PartitionSpec as P

MESH = pl.DeviceIdType.MESH
norm_epsilon = 1e-05
LANES = 128
HALF = 64
BF = jnp.bfloat16
F32 = jnp.float32


def nn(a, b):
    return lax.dot_general(a, b, (((1,), (0,)), ((), ())), preferred_element_type=F32)


def nt(a, b):
    return lax.dot_general(a, b, (((1,), (1,)), ((), ())), preferred_element_type=F32)


def wait_all(ref, sem):
    pltpu.make_async_copy(ref, ref, sem).wait()


def pack_pair(x, low):
    m = x.shape[0] // 2
    turned = pltpu.roll(x, HALF, 1)
    even = jnp.where(low[:m], x[:m], turned[m:])
    odd = jnp.where(low[:m], turned[:m], x[m:])
    return even.astype(BF), odd.astype(BF)


def unpack_pair(even, odd, low):
    m = even.shape[0]
    even, odd = even.astype(F32), odd.astype(F32)
    top = jnp.where(low[:m], even, pltpu.roll(odd, HALF, 1))
    bottom = jnp.where(low[:m], pltpu.roll(even, HALF, 1), odd)
    return jnp.concatenate([top, bottom], axis=0).astype(BF)


def pack_dense(x, lane):
    m = x.shape[0] // 4
    last = x[3 * m:]
    tail = jnp.concatenate([pltpu.roll(last, shift, 1) for shift in (96, 64, 32)], axis=0)
    return jnp.where(lane[:3 * m] < 96, x[:3 * m], tail).astype(BF)


def unpack_dense(packed, lane):
    m = packed.shape[0] // 3
    wide = packed.astype(F32)
    first, second, third = (
        pltpu.roll(wide[i * m:(i + 1) * m], 32 * (i + 1), 1) for i in range(3)
    )
    at = lane[:m]
    last = jnp.where(at < 32, first, jnp.where(at < 64, second, third))
    return jnp.concatenate([wide, last], axis=0).astype(BF)


def kernel(
    X, Z, G,
    lists_ref, bag_ref, feat_ref, table_ref, lcb_ref, projt_ref, fm_ref, gain_ref, cot_ref,
    inter_ref, tgrad_ref, lcbg_ref, projg_ref, fmg_ref,
    l1, r1, r1t, r2, bagl, feat_own, feat_in, oh, mt,
    sbuf0, sbuf1, rbuf0, rbuf1, wide0, wide1, pooled0, pooled1, esend0, esend1, erecv0, erecv1,
    pm, gsend, grecv, gt, hsend0, hsend1, hrecv0, hrecv1, tacc0, tacc1, jsend0, jsend1, jrecv0, jrecv1,
    w, k1, a2, k2, b3, k3, c4, k4, d5, k5, total,
    send_sem, list_sem, row_sem, grad_sem, grp_sem,
):
    S = X * Z * 2
    XC = X * 2
    groups = X * 2
    me_s = lax.axis_index("shard")
    me_g = lax.axis_index("grp")
    core = lax.rem(me_s, 2)
    me_z = lax.rem(lax.div(me_s, 2), Z)
    me_x = lax.div(me_s, 2 * Z)
    me_xc = me_x * 2 + core
    rows = table_ref.shape[1]
    width = table_ref.shape[0]
    features = lcb_ref.shape[0]
    samples, bags, slots = bag_ref.shape
    bag_lanes = bagl.shape[1]
    sbuf, rbuf, wide, pooled = (sbuf0, sbuf1), (rbuf0, rbuf1), (wide0, wide1), (pooled0, pooled1)
    esend, erecv = (esend0, esend1), (erecv0, erecv1)
    hsend, hrecv, tacc = (hsend0, hsend1), (hrecv0, hrecv1), (tacc0, tacc1)
    jsend, jrecv = (jsend0, jsend1), (jrecv0, jrecv1)
    cut = wide0.shape[0]
    parts = (slice(0, cut), slice(cut, width))

    def shard_of(x, z, c):
        return (x * Z + z) * 2 + c

    def peer(q, back):
        i = lax.rem(q, Z)
        j = lax.div(q, Z)
        dc = lax.rem(j, 2)
        dx = lax.rem(lax.div(j, 2) + i, X)
        if back:
            x, z = lax.rem(me_x + X - dx, X), lax.rem(me_z + Z - i, Z)
        else:
            x, z = lax.rem(me_x + dx, X), lax.rem(me_z + i, Z)
        return shard_of(x, z, lax.rem(core + dc, 2))

    def z_back(k):
        return shard_of(me_x, lax.rem(me_z + Z - k, Z), core)

    def xc_back(k):
        x = lax.rem(me_x + X - lax.div(k, 2), X)
        return shard_of(x, me_z, lax.rem(core + lax.rem(k, 2), 2))

    def group_back(k):
        return lax.rem(me_g + G - k, G)

    def group_ahead(k):
        return lax.rem(me_g + k, G)

    def send(src, dst, ssem, rsem, **where):
        pltpu.make_async_remote_copy(
            src_ref=src, dst_ref=dst, send_sem=ssem, recv_sem=rsem,
            device_id=where, device_id_type=MESH,
        ).start()

    def each(count, body, first=1):
        def step(k, carry):
            body(k)
            return carry

        lax.fori_loop(first, count, step, 0)

    barrier = pltpu.get_barrier_semaphore()

    def greet(**where):
        pl.semaphore_signal(barrier, inc=1, device_id=where, device_id_type=MESH)

    each(Z, lambda k: greet(shard=z_back(k)))
    each(XC, lambda k: greet(shard=xc_back(k)))
    each(G, lambda k: greet(grp=group_back(k)))

    lists = jnp.concatenate([lists_ref[...], lists_ref[...]], axis=1)
    for z in range(Z):
        for x in range(X):
            at = (x * Z + z) * 2
            l1[z, 2 * x:2 * x + 2, :] = lists[at:at + 2]

    feat_own[...] = jnp.full(feat_own.shape, -1, jnp.int32)
    for side in range(2):
        feat_own[:, 32 * side:32 * side + 32] = feat_ref[:, :32]
        feat_own[:, 64 + 16 * side:80 + 16 * side] = feat_ref[:, 32:48]
    pl.semaphore_wait(barrier, Z - 1 + XC - 1 + G - 1)

    r1[0] = l1[me_z]

    def send_list(k):
        z = lax.rem(me_z + Z - k, Z)
        send(l1.at[z], r1.at[k], send_sem.at[0], list_sem.at[0], shard=z_back(k))

    each(Z, send_list)
    each(G, lambda k: send(feat_own, feat_in.at[k], send_sem.at[1], grp_sem.at[0], grp=group_back(k)))
    feat_in[0] = feat_own[...]
    wait_all(r1.at[pl.ds(1, Z - 1)], list_sem.at[0])
    for xc in range(XC):
        for z in range(Z):
            r1t[xc, z:z + 1, :] = r1[z, xc:xc + 1, :]

    def send_list_on(k):
        xc = lax.rem(me_x + X - lax.div(k, 2), X) * 2 + lax.rem(core + lax.rem(k, 2), 2)
        send(r1t.at[xc], r2.at[k], send_sem.at[2], list_sem.at[1], shard=xc_back(k))

    each(XC, send_list_on)
    r2[0] = r1t[me_xc]
    wait_all(r2.at[pl.ds(1, XC - 1)], list_sem.at[1])

    low1 = lax.broadcasted_iota(jnp.int32, (1, LANES), 1) < HALF
    low = lax.broadcasted_iota(jnp.int32, (cut // 2, LANES), 1) < HALF
    lane = lax.broadcasted_iota(jnp.int32, (width, LANES), 1)
    row_line = lax.broadcasted_iota(jnp.int32, (256, LANES), 0)

    def serve(j, first):
        def want_of(i):
            return r2[lax.rem(lax.div(j, 2) + i, X) * 2 + lax.rem(j, 2), i:i + 1, :]

        for p in range(Z // 2):
            want = jnp.where(low1, want_of(2 * p), want_of(2 * p + 1))
            for kb in range(rows // 256):
                hit = jnp.where(row_line == want - kb * 256, 1.0, 0.0).astype(BF)
                oh[j, kb * 256:(kb + 1) * 256, p * LANES:(p + 1) * LANES] = hit
        found = nn(table_ref[...], oh[j])
        for p in range(Z // 2):
            for h in range(2):
                even, odd = pack_pair(found[parts[h], p * LANES:(p + 1) * LANES], low)
                sbuf[h][j * Z + 2 * p] = even
                sbuf[h][j * Z + 2 * p + 1] = odd

        each(j * Z + Z, lambda q: send(sbuf0.at[q], rbuf0.at[q], send_sem.at[3], row_sem.at[j],
                                       shard=peer(q, False)),
             first=j * Z + (1 if first else 0))

    serve(0, True)
    each(groups, lambda j: serve(j, False))
    each(S, lambda q: send(sbuf1.at[q], rbuf1.at[q], send_sem.at[4], row_sem.at[groups + lax.div(q, Z)],
                           shard=peer(q, False)))
    for h in range(2):
        rbuf[h][0] = sbuf[h][0]

    bagl[...] = jnp.full(bagl.shape, -1, jnp.int32)
    for n in range(samples):
        at = n // 2 * LANES
        side = n % 2
        bagl[:, at + 32 * side:at + 32 * side + 32] = bag_ref[n, :, :32]
        bagl[:, at + 64 + 16 * side:at + 80 + 16 * side] = bag_ref[n, :, 32:48]
    slot_line = lax.broadcasted_iota(jnp.int32, (HALF, LANES), 0)

    def count(j):
        for i in range(Z):
            base = peer(j * Z + i, True) * HALF
            for c in range(bag_lanes // LANES):
                lanes = slice(c * LANES, (c + 1) * LANES)
                times = jnp.zeros((HALF, LANES), F32)
                for b in range(bags):
                    times = times + jnp.where(slot_line == bagl[b:b + 1, lanes] - base, 1.0, 0.0)
                mt[j, i * HALF:(i + 1) * HALF, lanes] = times.astype(BF)

    each(groups, count, first=0)

    wait_all(feat_in.at[pl.ds(1, G - 1)], grp_sem.at[0])
    feat_line = lax.broadcasted_iota(jnp.int32, (features, LANES), 0)
    lane1 = lax.broadcasted_iota(jnp.int32, (1, LANES), 1)
    second = ((lane1 >= 32) & (lane1 < 64)) | ((lane1 >= 80) & (lane1 < 96))
    for k in range(G):
        held = feat_line == feat_in[k]
        pm[:features, k * LANES:(k + 1) * LANES] = jnp.where(held & ~second, 1.0, 0.0).astype(BF)
        pm[features:, k * LANES:(k + 1) * LANES] = jnp.where(held & second, 1.0, 0.0).astype(BF)
    eye = jnp.where(
        lax.broadcasted_iota(jnp.int32, (width, width), 0) == lax.broadcasted_iota(jnp.int32, (width, width), 1),
        1.0, 0.0,
    )
    fm = fm_ref[...]
    fmt = nt(eye.astype(BF), fm).astype(BF)
    gain = jnp.sum(eye * gain_ref[...], axis=1, keepdims=True)

    def pool(h, j, first):
        at = j * Z
        if first:
            wait_all(rbuf[h].at[pl.ds(1, Z - 1)], row_sem.at[h * groups + j])
        else:
            wait_all(rbuf[h].at[pl.ds(at, Z)], row_sem.at[h * groups + j])
        for p in range(Z // 2):
            wide[h][:, p * LANES:(p + 1) * LANES] = unpack_pair(
                rbuf[h][at + 2 * p], rbuf[h][at + 2 * p + 1], low
            )
        now = nn(wide[h][...], mt[j])
        pooled[h][...] = now if first else pooled[h][...] + now

    for h in range(2):
        pool(h, 0, True)
        each(groups, lambda j, h=h: pool(h, j, False))
        for g in range(G):
            esend[h][group_back(g)] = pack_dense(pooled[h][:, g * LANES:(g + 1) * LANES], lane)
        each(G, lambda k, h=h: send(esend[h].at[k], erecv[h].at[k], send_sem.at[5 + h], grp_sem.at[1 + h],
                                    grp=group_back(k)))
        erecv[h][0] = esend[h][0]
    for h in range(2):
        wait_all(erecv[h].at[pl.ds(1, G - 1)], grp_sem.at[1 + h])

    arrived = jnp.concatenate([
        jnp.concatenate([unpack_dense(erecv[h][k], lane) for h in range(2)], axis=0) for k in range(G)
    ], axis=1)
    both = nt(arrived, pm[...]).astype(BF)
    lcb = lcb_ref[...]
    projt = projt_ref[...]
    lcb_grad = jnp.zeros((features, features), F32)
    proj_grad = jnp.zeros(projt.shape, F32)
    fm_grad = jnp.zeros(fm.shape, F32)
    grads_in = []
    for n in range(2):
        xt = both[:, n * features:(n + 1) * features]
        x = nt(pm[n * features:(n + 1) * features, :], arrived).astype(BF)
        low_rank = nt(xt, projt).astype(BF)
        low_rank_t = nt(projt, xt).astype(BF)
        crossed_t = nn(low_rank_t, xt).astype(BF)
        summed = xt.astype(F32) + nn(xt, lcb) + nn(fmt, crossed_t)
        center = summed - jnp.mean(summed, axis=0, keepdims=True)
        inv_std = lax.rsqrt(jnp.mean(center * center, axis=0, keepdims=True) + norm_epsilon)
        normed = center * inv_std
        inter_ref[n] = (normed * gain).astype(BF)
        scaled = cot_ref[n].astype(F32) * gain
        grad_sum = inv_std * (
            scaled
            - jnp.mean(scaled, axis=0, keepdims=True)
            - normed * jnp.mean(scaled * normed, axis=0, keepdims=True)
        )
        grad_low = grad_sum.astype(BF)
        grad_cross_t = nn(fm, grad_low).astype(BF)
        grad_proj = nt(xt, grad_cross_t).astype(BF)
        grad_proj_t = nt(grad_cross_t, xt).astype(BF)
        fm_grad = fm_grad + nt(crossed_t, grad_low)
        proj_grad = proj_grad + nn(grad_proj_t, xt)
        lcb_grad = lcb_grad + nn(x, grad_low)
        grads_in.append((
            grad_sum + nt(grad_low, lcb) + nn(low_rank, grad_cross_t) + nn(grad_proj, projt)
        ).astype(BF))

    back = nn(jnp.concatenate(grads_in, axis=1), pm[...])
    for k in range(G):
        gsend[k] = pack_dense(back[:, k * LANES:(k + 1) * LANES], lane)
    each(G, lambda k: send(gsend.at[k], grecv.at[k], send_sem.at[7], grp_sem.at[3], grp=group_ahead(k)))
    grecv[0] = gsend[0]

    chunk = a2.shape[1]
    span = Z * chunk
    total[...] = jnp.zeros_like(total)
    total[:features] = lcb_grad
    total[features:features + HALF] = proj_grad
    total[features + HALF:features + 2 * HALF, :width] = fm_grad
    for g in range(G):
        w[g] = total[g * span:(g + 1) * span].astype(BF)
    each(G, lambda k: send(w.at[group_back(k)], k1.at[k], send_sem.at[8], grp_sem.at[4], grp=group_back(k)))

    wait_all(grecv.at[pl.ds(1, G - 1)], grp_sem.at[3])
    for g in range(G):
        gt[:, g * LANES:(g + 1) * LANES] = unpack_dense(grecv[group_back(g)], lane)

    def give(j, first):
        slot_grad = nt(gt[...], mt[j])
        for p in range(Z // 2):
            for h in range(2):
                even, odd = pack_pair(slot_grad[parts[h], p * LANES:(p + 1) * LANES], low)
                hsend[h][j * Z + 2 * p] = even
                hsend[h][j * Z + 2 * p + 1] = odd

        each(j * Z + Z, lambda q: send(hsend0.at[q], hrecv0.at[q], send_sem.at[9], grad_sem.at[j],
                                       shard=peer(q, True)),
             first=j * Z + (1 if first else 0))

    def give_some(step, steps):
        first = step * groups // steps
        last = (step + 1) * groups // steps
        if first == 0:
            give(0, True)
            first = 1
        each(last, lambda j: give(j, False), first=first)

    give_some(0, 4)
    wait_all(k1.at[pl.ds(1, G - 1)], grp_sem.at[4])
    part = w[me_g].astype(F32)
    for k in range(1, G):
        part = part + k1[k].astype(F32)
    for z in range(Z):
        a2[z] = part[z * chunk:(z + 1) * chunk]
    each(Z, lambda k: send(a2.at[lax.rem(me_z + Z - k, Z)], k2.at[k], send_sem.at[10], grp_sem.at[5],
                           shard=z_back(k)))

    give_some(1, 4)
    wait_all(k2.at[pl.ds(1, Z - 1)], grp_sem.at[5])
    part = a2[me_z]
    for k in range(1, Z):
        part = part + k2[k]
    b3[...] = part
    k3[0] = part
    each(XC, lambda k: send(b3, k3.at[k], send_sem.at[11], grp_sem.at[6], shard=xc_back(k)))

    give_some(2, 4)
    wait_all(k3.at[pl.ds(1, XC - 1)], grp_sem.at[6])

    def from_xc(s):
        dx = lax.rem(s // 2 + X - me_x, X)
        return k3[dx * 2 + lax.rem(s % 2 + core, 2)]

    part = from_xc(0)
    for s in range(1, XC):
        part = part + from_xc(s)
    c4[...] = part
    k4[0] = part
    each(Z, lambda k: send(c4, k4.at[k], send_sem.at[12], grp_sem.at[7], shard=z_back(k)))

    give_some(3, 4)
    each(S, lambda q: send(hsend1.at[q], hrecv1.at[q], send_sem.at[13], grad_sem.at[groups + lax.div(q, Z)],
                           shard=peer(q, True)))
    for h in range(2):
        hrecv[h][0] = hsend[h][0]

    wait_all(k4.at[pl.ds(1, Z - 1)], grp_sem.at[7])
    for z in range(Z):
        d5[z * chunk:(z + 1) * chunk] = k4[lax.rem(z + Z - me_z, Z)].astype(BF)
    k5[0] = d5[...]
    each(G, lambda k: send(d5, k5.at[k], send_sem.at[14], grp_sem.at[8], grp=group_back(k)))

    per = rows // G

    def take(h, j, first):
        at = j * Z
        if first:
            wait_all(hrecv[h].at[pl.ds(1, Z - 1)], grad_sem.at[h * groups + j])
        else:
            wait_all(hrecv[h].at[pl.ds(at, Z)], grad_sem.at[h * groups + j])
        for p in range(Z // 2):
            wide[h][:, p * LANES:(p + 1) * LANES] = unpack_pair(
                hrecv[h][at + 2 * p], hrecv[h][at + 2 * p + 1], low
            )
        for g in range(G):
            now = nt(wide[h][...], oh[j, g * per:(g + 1) * per, :])
            tacc[h][g] = now if first else tacc[h][g] + now

    def send_table(k, h):
        to = group_back(k)
        jsend[h][k] = tacc[h][to].astype(BF)
        send(jsend[h].at[k], jrecv[h].at[k], send_sem.at[15 + h], grp_sem.at[9 + h], grp=to)

    for h in range(2):
        take(h, 0, True)
        each(groups, lambda j, h=h: take(h, j, False))
        each(G, lambda k, h=h: send_table(k, h))

    wait_all(k5.at[pl.ds(1, G - 1)], grp_sem.at[8])
    for g in range(G):
        total[g * span:(g + 1) * span] = k5[lax.rem(g + G - me_g, G)].astype(F32)
    lcbg_ref[...] = total[:features]
    projg_ref[...] = total[features:features + HALF]
    fmg_ref[...] = total[features + HALF:features + 2 * HALF, :width]

    for h in range(2):
        wait_all(jrecv[h].at[pl.ds(1, G - 1)], grp_sem.at[9 + h])
        out = tacc[h][me_g]
        for k in range(1, G):
            out = out + jrecv[h][k].astype(F32)
        tgrad_ref[parts[h], :] = out

    wait_all(r1.at[pl.ds(1, Z - 1)], send_sem.at[0])
    wait_all(feat_in.at[pl.ds(1, G - 1)], send_sem.at[1])
    wait_all(r2.at[pl.ds(1, XC - 1)], send_sem.at[2])
    wait_all(sbuf0.at[pl.ds(1, S - 1)], send_sem.at[3])
    wait_all(sbuf1.at[pl.ds(1, S - 1)], send_sem.at[4])
    wait_all(esend0.at[pl.ds(1, G - 1)], send_sem.at[5])
    wait_all(esend1.at[pl.ds(1, G - 1)], send_sem.at[6])
    wait_all(gsend.at[pl.ds(1, G - 1)], send_sem.at[7])
    wait_all(k1.at[pl.ds(1, G - 1)], send_sem.at[8])
    wait_all(hsend0.at[pl.ds(1, S - 1)], send_sem.at[9])
    wait_all(k2.at[pl.ds(1, Z - 1)], send_sem.at[10])
    wait_all(k3.at[pl.ds(1, XC - 1)], send_sem.at[11])
    wait_all(k4.at[pl.ds(1, Z - 1)], send_sem.at[12])
    wait_all(hsend1.at[pl.ds(1, S - 1)], send_sem.at[13])
    wait_all(k5.at[pl.ds(1, G - 1)], send_sem.at[14])
    wait_all(jsend0.at[pl.ds(1, G - 1)], send_sem.at[15])
    wait_all(jsend1.at[pl.ds(1, G - 1)], send_sem.at[16])


def hand_over(*refs):
    half = len(refs) // 2
    for i in range(half):
        refs[half + i][...] = refs[i][...]


def shards(X, Z, emb_table, touched, bag_slots, feat_of_slot, lcb_weight, proj_weight, fm_weight,
           ln_gain, cotangent):
    G = lax.axis_size("grp")
    S = X * Z * 2
    XC = X * 2
    samples, slots, bags = bag_slots.shape
    table_t = emb_table.T
    width, rows = table_t.shape
    features = lcb_weight.shape[0]
    rank = proj_weight.shape[1]
    groups = X * 2
    bag_lanes = samples // 2 * LANES
    chunk = -(-(features + 2 * HALF) // (G * Z * 8)) * 8
    cut = width * 2 // 3
    heights = (cut, width - cut)
    vm = pltpu.VMEM
    dma = pltpu.SemaphoreType.DMA
    per = rows // G

    def two(shape_of, kind):
        return [vm(shape_of(height), kind) for height in heights]

    scratch = [
        vm((Z, XC, LANES), jnp.int32),
        vm((Z, XC, LANES), jnp.int32),
        vm((XC, Z, LANES), jnp.int32),
        vm((XC, Z, LANES), jnp.int32),
        vm((bags, bag_lanes), jnp.int32),
        vm((1, LANES), jnp.int32),
        vm((G, 1, LANES), jnp.int32),
        vm((groups, rows, Z * HALF), BF),
        vm((groups, Z * HALF, bag_lanes), BF),
        *two(lambda m: (S, m // 2, LANES), BF),
        *two(lambda m: (S, m // 2, LANES), BF),
        *two(lambda m: (m, Z * HALF), BF),
        *two(lambda m: (m, bag_lanes), F32),
        *two(lambda m: (G, m * 3 // 4, LANES), BF),
        *two(lambda m: (G, m * 3 // 4, LANES), BF),
        vm((2 * features, G * LANES), BF),
        vm((G, width * 3 // 4, LANES), BF),
        vm((G, width * 3 // 4, LANES), BF),
        vm((width, bag_lanes), BF),
        *two(lambda m: (S, m // 2, LANES), BF),
        *two(lambda m: (S, m // 2, LANES), BF),
        *two(lambda m: (G, m, per), F32),
        *two(lambda m: (G, m, per), BF),
        *two(lambda m: (G, m, per), BF),
        vm((G, Z * chunk, features), BF),
        vm((G, Z * chunk, features), BF),
        vm((Z, chunk, features), F32),
        vm((Z, chunk, features), F32),
        vm((chunk, features), F32),
        vm((XC, chunk, features), F32),
        vm((chunk, features), F32),
        vm((Z, chunk, features), F32),
        vm((Z * chunk, features), BF),
        vm((G, Z * chunk, features), BF),
        vm((G * Z * chunk, features), F32),
        dma((17,)),
        dma((2,)),
        dma((2 * groups,)),
        dma((2 * groups,)),
        dma((11,)),
    ]
    whole = pl.BlockSpec(memory_space=pltpu.VMEM)
    shapes = (
        jax.ShapeDtypeStruct((2, width, features), BF),
        jax.ShapeDtypeStruct((width, per), F32),
        jax.ShapeDtypeStruct((features, features), F32),
        jax.ShapeDtypeStruct((rank, features), F32),
        jax.ShapeDtypeStruct((rank, width), F32),
    )
    results = pl.pallas_call(
        functools.partial(kernel, X, Z, G),
        out_shape=shapes,
        in_specs=[whole] * 9,
        out_specs=[whole] * 5,
        scratch_shapes=scratch,
        compiler_params=pltpu.CompilerParams(
            collective_id=0, has_side_effects=True, vmem_limit_bytes=58 * 1024 * 1024
        ),
    )(
        touched.reshape(S, HALF), jnp.transpose(bag_slots, (0, 2, 1)), feat_of_slot, table_t, lcb_weight,
        proj_weight.T, fm_weight, ln_gain.reshape(1, -1), jnp.transpose(cotangent, (0, 2, 1)),
    )
    inter, tgrad, lcbg, projg, fmg = pl.pallas_call(
        hand_over,
        out_shape=shapes,
        in_specs=[whole] * 5,
        out_specs=[whole] * 5,
    )(*results)
    return (jnp.transpose(inter, (0, 2, 1)), tgrad.T, lcbg, projg.T, fmg)


def solution(mesh):
    S = mesh.shape["shard"]
    Z = mesh.shape["grp"]
    X = S // (2 * Z)
    placed = (
        P("shard", None),
        P("shard", "grp", None, None),
        P("shard", "grp", None),
        P("grp", None),
        P(),
        P(),
        P(),
        P(),
        P(("shard", "grp"), None, None),
    )
    return jax.shard_map(
        functools.partial(shards, X, Z),
        mesh=mesh,
        in_specs=placed,
        out_specs=(P(("shard", "grp"), None, None), P(("shard", "grp"), None), P(), P(), P()),
        check_vma=False,
    )
```

```python
import functools

import jax
import jax.numpy as jnp
from jax import lax
from jax.experimental import pallas as pl
from jax.experimental.pallas import tpu as pltpu
from jax.sharding import PartitionSpec as P

MESH = pl.DeviceIdType.MESH
norm_epsilon = 1e-05
LANES = 128
HALF = 64
BF = jnp.bfloat16
F32 = jnp.float32


def nn(a, b):
    return lax.dot_general(a, b, (((1,), (0,)), ((), ())), preferred_element_type=F32)


def nt(a, b):
    return lax.dot_general(a, b, (((1,), (1,)), ((), ())), preferred_element_type=F32)


def wait_all(ref, sem):
    pltpu.make_async_copy(ref, ref, sem).wait()


def pack_pair(x, low):
    m = x.shape[0] // 2
    turned = pltpu.roll(x, HALF, 1)
    even = jnp.where(low[:m], x[:m], turned[m:])
    odd = jnp.where(low[:m], turned[:m], x[m:])
    return even.astype(BF), odd.astype(BF)


def unpack_pair(even, odd, low):
    m = even.shape[0]
    even, odd = even.astype(F32), odd.astype(F32)
    top = jnp.where(low[:m], even, pltpu.roll(odd, HALF, 1))
    bottom = jnp.where(low[:m], pltpu.roll(even, HALF, 1), odd)
    return jnp.concatenate([top, bottom], axis=0).astype(BF)


def pack_dense(x, lane):
    m = x.shape[0] // 4
    last = x[3 * m:]
    tail = jnp.concatenate([pltpu.roll(last, shift, 1) for shift in (96, 64, 32)], axis=0)
    return jnp.where(lane[:3 * m] < 96, x[:3 * m], tail).astype(BF)


def unpack_dense(packed, lane):
    m = packed.shape[0] // 3
    wide = packed.astype(F32)
    first, second, third = (
        pltpu.roll(wide[i * m:(i + 1) * m], 32 * (i + 1), 1) for i in range(3)
    )
    at = lane[:m]
    last = jnp.where(at < 32, first, jnp.where(at < 64, second, third))
    return jnp.concatenate([wide, last], axis=0).astype(BF)


def kernel(
    X, Z, G,
    lists_ref, bag_ref, feat_ref, table_ref, lcb_ref, projt_ref, fm_ref, gain_ref, cot_ref,
    inter_ref, tgrad_ref, lcbg_ref, projg_ref, fmg_ref,
    l1, r1, r1t, r2, bagl, feat_own, feat_in, oh, mt,
    sbuf0, sbuf1, rbuf0, rbuf1, wide0, wide1, pooled0, pooled1, esend0, esend1, erecv0, erecv1,
    pm, gsend0, gsend1, grecv0, grecv1, gt, hsend0, hsend1, hsend2, hrecv0, hrecv1, hrecv2,
    tacc0, tacc1, tacc2, jsend0, jsend1, jsend2, jrecv0, jrecv1, jrecv2,
    w, k1, a2, k2, b3, k3, c4, k4, d5, k5, total,
    send_sem, list_sem, row_sem, grad_sem, grp_sem,
):
    S = X * Z * 2
    XC = X * 2
    groups = X * 2
    me_s = lax.axis_index("shard")
    me_g = lax.axis_index("grp")
    core = lax.rem(me_s, 2)
    me_z = lax.rem(lax.div(me_s, 2), Z)
    me_x = lax.div(me_s, 2 * Z)
    me_xc = me_x * 2 + core
    rows = table_ref.shape[1]
    width = table_ref.shape[0]
    features = lcb_ref.shape[0]
    samples, bags, slots = bag_ref.shape
    bag_lanes = bagl.shape[1]
    sbuf, rbuf, wide, pooled = (sbuf0, sbuf1), (rbuf0, rbuf1), (wide0, wide1), (pooled0, pooled1)
    esend, erecv = (esend0, esend1), (erecv0, erecv1)
    gsend, grecv = (gsend0, gsend1), (grecv0, grecv1)
    hsend, hrecv, tacc = (hsend0, hsend1, hsend2), (hrecv0, hrecv1, hrecv2), (tacc0, tacc1, tacc2)
    jsend, jrecv = (jsend0, jsend1, jsend2), (jrecv0, jrecv1, jrecv2)
    lead = tacc0.shape[1]
    mid = lead + tacc1.shape[1]
    back_parts = (slice(0, lead), slice(lead, width))
    grad_parts = (slice(0, lead), slice(lead, mid), slice(mid, width))
    cut = wide0.shape[0]
    parts = (slice(0, cut), slice(cut, width))

    def shard_of(x, z, c):
        return (x * Z + z) * 2 + c

    def peer(q, back):
        i = lax.rem(q, Z)
        j = lax.div(q, Z)
        dc = lax.rem(j, 2)
        dx = lax.div(j, 2)
        if back:
            x, z = lax.rem(me_x + X - dx, X), lax.rem(me_z + Z - i, Z)
        else:
            x, z = lax.rem(me_x + dx, X), lax.rem(me_z + i, Z)
        return shard_of(x, z, lax.rem(core + dc, 2))

    def z_back(k):
        return shard_of(me_x, lax.rem(me_z + Z - k, Z), core)

    def xc_back(k):
        x = lax.rem(me_x + X - lax.div(k, 2), X)
        return shard_of(x, me_z, lax.rem(core + lax.rem(k, 2), 2))

    def group_back(k):
        return lax.rem(me_g + G - k, G)

    def group_ahead(k):
        return lax.rem(me_g + k, G)

    def send(src, dst, ssem, rsem, **where):
        pltpu.make_async_remote_copy(
            src_ref=src, dst_ref=dst, send_sem=ssem, recv_sem=rsem,
            device_id=where, device_id_type=MESH,
        ).start()

    def each(count, body, first=1):
        def step(k, carry):
            body(k)
            return carry

        lax.fori_loop(first, count, step, 0)

    barrier = pltpu.get_barrier_semaphore()

    def greet(**where):
        pl.semaphore_signal(barrier, inc=1, device_id=where, device_id_type=MESH)

    each(Z, lambda k: greet(shard=z_back(k)))
    each(XC, lambda k: greet(shard=xc_back(k)))
    each(G, lambda k: greet(grp=group_back(k)))

    lists = jnp.concatenate([lists_ref[...], lists_ref[...]], axis=1)
    for z in range(Z):
        for x in range(X):
            at = (x * Z + z) * 2
            l1[z, 2 * x:2 * x + 2, :] = lists[at:at + 2]

    feat_own[...] = jnp.full(feat_own.shape, -1, jnp.int32)
    for side in range(2):
        feat_own[:, 32 * side:32 * side + 32] = feat_ref[:, :32]
        feat_own[:, 64 + 16 * side:80 + 16 * side] = feat_ref[:, 32:48]
    pl.semaphore_wait(barrier, Z - 1 + XC - 1 + G - 1)

    r1[0] = l1[me_z]

    def send_list(k):
        z = lax.rem(me_z + Z - k, Z)
        send(l1.at[z], r1.at[k], send_sem.at[0], list_sem.at[0], shard=z_back(k))

    each(Z, send_list)
    each(G, lambda k: send(feat_own, feat_in.at[k], send_sem.at[1], grp_sem.at[0], grp=group_back(k)))
    feat_in[0] = feat_own[...]
    wait_all(r1.at[pl.ds(1, Z - 1)], list_sem.at[0])
    for xc in range(XC):
        for z in range(Z):
            r1t[xc, z:z + 1, :] = r1[z, xc:xc + 1, :]

    def send_list_on(k):
        xc = lax.rem(me_x + X - lax.div(k, 2), X) * 2 + lax.rem(core + lax.rem(k, 2), 2)
        send(r1t.at[xc], r2.at[k], send_sem.at[2], list_sem.at[k], shard=xc_back(k))

    each(XC, send_list_on)
    r2[0] = r1t[me_xc]

    low1 = lax.broadcasted_iota(jnp.int32, (1, LANES), 1) < HALF
    low = lax.broadcasted_iota(jnp.int32, (cut // 2, LANES), 1) < HALF
    lane = lax.broadcasted_iota(jnp.int32, (width, LANES), 1)
    row_line = lax.broadcasted_iota(jnp.int32, (256, LANES), 0)

    def serve(j, first):
        if not first:
            wait_all(r2.at[j], list_sem.at[j])
        for p in range(Z // 2):
            want = jnp.where(low1, r2[j, 2 * p:2 * p + 1, :], r2[j, 2 * p + 1:2 * p + 2, :])
            for kb in range(rows // 256):
                hit = jnp.where(row_line == want - kb * 256, 1.0, 0.0).astype(BF)
                oh[j, kb * 256:(kb + 1) * 256, p * LANES:(p + 1) * LANES] = hit
        found = nn(table_ref[...], oh[j])
        for p in range(Z // 2):
            for h in range(2):
                even, odd = pack_pair(found[parts[h], p * LANES:(p + 1) * LANES], low)
                sbuf[h][j * Z + 2 * p] = even
                sbuf[h][j * Z + 2 * p + 1] = odd

        each(j * Z + Z, lambda q: send(sbuf0.at[q], rbuf0.at[q], send_sem.at[3], row_sem.at[j],
                                       shard=peer(q, False)),
             first=j * Z + (1 if first else 0))

    serve(0, True)
    each(groups, lambda j: serve(j, False))
    each(S, lambda q: send(sbuf1.at[q], rbuf1.at[q], send_sem.at[4], row_sem.at[groups + lax.div(q, Z)],
                           shard=peer(q, False)))
    for h in range(2):
        rbuf[h][0] = sbuf[h][0]

    bagl[...] = jnp.full(bagl.shape, -1, jnp.int32)
    for n in range(samples):
        at = n // 2 * LANES
        side = n % 2
        bagl[:, at + 32 * side:at + 32 * side + 32] = bag_ref[n, :, :32]
        bagl[:, at + 64 + 16 * side:at + 80 + 16 * side] = bag_ref[n, :, 32:48]
    slot_line = lax.broadcasted_iota(jnp.int32, (HALF, LANES), 0)

    def count(j):
        for i in range(Z):
            base = peer(j * Z + i, True) * HALF
            for c in range(bag_lanes // LANES):
                lanes = slice(c * LANES, (c + 1) * LANES)
                times = jnp.zeros((HALF, LANES), F32)
                for b in range(bags):
                    times = times + jnp.where(slot_line == bagl[b:b + 1, lanes] - base, 1.0, 0.0)
                mt[j, i * HALF:(i + 1) * HALF, lanes] = times.astype(BF)

    each(groups, count, first=0)

    wait_all(feat_in.at[pl.ds(1, G - 1)], grp_sem.at[0])
    feat_line = lax.broadcasted_iota(jnp.int32, (features, LANES), 0)
    lane1 = lax.broadcasted_iota(jnp.int32, (1, LANES), 1)
    second = ((lane1 >= 32) & (lane1 < 64)) | ((lane1 >= 80) & (lane1 < 96))
    for k in range(G):
        held = feat_line == feat_in[k]
        pm[:features, k * LANES:(k + 1) * LANES] = jnp.where(held & ~second, 1.0, 0.0).astype(BF)
        pm[features:, k * LANES:(k + 1) * LANES] = jnp.where(held & second, 1.0, 0.0).astype(BF)
    eye = jnp.where(
        lax.broadcasted_iota(jnp.int32, (width, width), 0) == lax.broadcasted_iota(jnp.int32, (width, width), 1),
        1.0, 0.0,
    )
    fm = fm_ref[...]
    fmt = nt(eye.astype(BF), fm).astype(BF)
    gain = jnp.sum(eye * gain_ref[...], axis=1, keepdims=True)

    def pool(h, j, first):
        at = j * Z
        if first:
            wait_all(rbuf[h].at[pl.ds(1, Z - 1)], row_sem.at[h * groups + j])
        else:
            wait_all(rbuf[h].at[pl.ds(at, Z)], row_sem.at[h * groups + j])
        for p in range(Z // 2):
            wide[h][:, p * LANES:(p + 1) * LANES] = unpack_pair(
                rbuf[h][at + 2 * p], rbuf[h][at + 2 * p + 1], low
            )
        now = nn(wide[h][...], mt[j])
        pooled[h][...] = now if first else pooled[h][...] + now

    for h in range(2):
        pool(h, 0, True)
        each(groups, lambda j, h=h: pool(h, j, False))
        for g in range(G):
            esend[h][group_back(g)] = pack_dense(pooled[h][:, g * LANES:(g + 1) * LANES], lane)
        each(G, lambda k, h=h: send(esend[h].at[k], erecv[h].at[k], send_sem.at[5 + h], grp_sem.at[1 + h],
                                    grp=group_back(k)))
        erecv[h][0] = esend[h][0]
    for h in range(2):
        wait_all(erecv[h].at[pl.ds(1, G - 1)], grp_sem.at[1 + h])

    arrived = jnp.concatenate([
        jnp.concatenate([unpack_dense(erecv[h][k], lane) for h in range(2)], axis=0) for k in range(G)
    ], axis=1)
    both = nt(arrived, pm[...]).astype(BF)
    lcb = lcb_ref[...]
    projt = projt_ref[...]
    grads_in = []
    later = []
    for n in range(2):
        xt = both[:, n * features:(n + 1) * features]
        low_rank = nt(xt, projt).astype(BF)
        low_rank_t = nt(projt, xt).astype(BF)
        crossed_t = nn(low_rank_t, xt).astype(BF)
        summed = xt.astype(F32) + nn(xt, lcb) + nn(fmt, crossed_t)
        center = summed - jnp.mean(summed, axis=0, keepdims=True)
        inv_std = lax.rsqrt(jnp.mean(center * center, axis=0, keepdims=True) + norm_epsilon)
        normed = center * inv_std
        inter_ref[n] = (normed * gain).astype(BF)
        scaled = cot_ref[n].astype(F32) * gain
        grad_sum = inv_std * (
            scaled
            - jnp.mean(scaled, axis=0, keepdims=True)
            - normed * jnp.mean(scaled * normed, axis=0, keepdims=True)
        )
        grad_low = grad_sum.astype(BF)
        grad_cross_t = nn(fm, grad_low).astype(BF)
        grad_proj = nt(xt, grad_cross_t).astype(BF)
        grads_in.append((
            grad_sum + nt(grad_low, lcb) + nn(low_rank, grad_cross_t) + nn(grad_proj, projt)
        ).astype(BF))
        later.append((xt, crossed_t, grad_low, grad_cross_t))

    grad_in = jnp.concatenate(grads_in, axis=1)

    def send_back(h):
        back = nn(grad_in[back_parts[h]], pm[...])
        for k in range(G):
            gsend[h][k] = pack_dense(back[:, k * LANES:(k + 1) * LANES], lane)
        each(G, lambda k: send(gsend[h].at[k], grecv[h].at[k], send_sem.at[7 + h], grp_sem.at[3 + h],
                               grp=group_ahead(k)))
        grecv[h][0] = gsend[h][0]

    send_back(0)

    lcb_grad = jnp.zeros((features, features), F32)
    proj_grad = jnp.zeros(projt.shape, F32)
    fm_grad = jnp.zeros(fm.shape, F32)
    for n in range(2):
        xt, crossed_t, grad_low, grad_cross_t = later[n]
        x = nt(pm[n * features:(n + 1) * features, :], arrived).astype(BF)
        grad_proj_t = nt(grad_cross_t, xt).astype(BF)
        fm_grad = fm_grad + nt(crossed_t, grad_low)
        proj_grad = proj_grad + nn(grad_proj_t, xt)
        lcb_grad = lcb_grad + nn(x, grad_low)
    chunk = a2.shape[1]
    span = w.shape[1]
    total[...] = jnp.zeros_like(total)
    total[:features] = lcb_grad
    total[features:features + HALF] = proj_grad
    total[features + HALF:features + 2 * HALF, :width] = fm_grad
    for g in range(G):
        w[g] = total[g * span:(g + 1) * span].astype(BF)
    each(G, lambda k: send(w.at[group_back(k)], k1.at[k], send_sem.at[9], grp_sem.at[5], grp=group_back(k)))
    send_back(1)

    def bring(h):
        wait_all(grecv[h].at[pl.ds(1, G - 1)], grp_sem.at[3 + h])
        for g in range(G):
            gt[back_parts[h], g * LANES:(g + 1) * LANES] = unpack_dense(grecv[h][group_back(g)], lane)

    bring(0)

    def give(h, j, first):
        slot_grad = nt(gt[grad_parts[h], :], mt[j])
        for p in range(Z // 2):
            even, odd = pack_pair(slot_grad[:, p * LANES:(p + 1) * LANES], low)
            hsend[h][j * Z + 2 * p] = even
            hsend[h][j * Z + 2 * p + 1] = odd
        if first:
            hrecv[h][0] = hsend[h][0]
        each(j * Z + Z, lambda q: send(hsend[h].at[q], hrecv[h].at[q], send_sem.at[10 + h],
                                       grad_sem.at[h * groups + j], shard=peer(q, True)),
             first=j * Z + (1 if first else 0))

    def give_some(h, first, last):
        if first == 0:
            give(h, 0, True)
            first = 1
        each(last, lambda j: give(h, j, False), first=first)

    per = rows // G

    def take(h, j, first):
        at = j * Z
        if first:
            wait_all(hrecv[h].at[pl.ds(1, Z - 1)], grad_sem.at[h * groups + j])
        else:
            wait_all(hrecv[h].at[pl.ds(at, Z)], grad_sem.at[h * groups + j])
        m = tacc[h].shape[1]
        for p in range(Z // 2):
            wide0[:m, p * LANES:(p + 1) * LANES] = unpack_pair(
                hrecv[h][at + 2 * p], hrecv[h][at + 2 * p + 1], low
            )
        for g in range(G):
            now = nt(wide0[:m, :], oh[j, g * per:(g + 1) * per, :])
            tacc[h][g] = now if first else tacc[h][g] + now

    def take_all(h):
        take(h, 0, True)
        each(groups, lambda j: take(h, j, False))

        def send_table(k):
            to = group_back(k)
            jsend[h][k] = tacc[h][to].astype(BF)
            send(jsend[h].at[k], jrecv[h].at[k], send_sem.at[13 + h], grp_sem.at[6 + h], grp=to)

        each(G, send_table)

    give_some(0, 0, groups)
    wait_all(k1.at[pl.ds(1, G - 1)], grp_sem.at[5])
    part = w[me_g].astype(F32)
    for k in range(1, G):
        part = part + k1[k].astype(F32)
    a2[...] = jnp.zeros_like(a2)
    for z in range(span // chunk):
        a2[z] = part[z * chunk:(z + 1) * chunk]
    each(Z, lambda k: send(a2.at[lax.rem(me_z + Z - k, Z)], k2.at[k], send_sem.at[16], grp_sem.at[9],
                           shard=z_back(k)))
    bring(1)
    third = groups * 3 // 8
    give_some(1, 0, third)
    take_all(0)

    wait_all(k2.at[pl.ds(1, Z - 1)], grp_sem.at[9])
    part = a2[me_z]
    for k in range(1, Z):
        part = part + k2[k]
    b3[...] = part
    k3[0] = part
    each(XC, lambda k: send(b3, k3.at[k], send_sem.at[17], grp_sem.at[10], shard=xc_back(k)))

    give_some(1, third, 2 * third)
    wait_all(k3.at[pl.ds(1, XC - 1)], grp_sem.at[10])

    def from_xc(s):
        dx = lax.rem(s // 2 + X - me_x, X)
        return k3[dx * 2 + lax.rem(s % 2 + core, 2)]

    part = from_xc(0)
    for s in range(1, XC):
        part = part + from_xc(s)
    c4[...] = part
    k4[0] = part
    each(Z, lambda k: send(c4, k4.at[k], send_sem.at[18], grp_sem.at[11], shard=z_back(k)))

    give_some(1, 2 * third, groups)
    give_some(2, 0, groups)

    wait_all(k4.at[pl.ds(1, Z - 1)], grp_sem.at[11])
    for z in range(span // chunk):
        d5[z * chunk:(z + 1) * chunk] = k4[lax.rem(z + Z - me_z, Z)].astype(BF)
    k5[0] = d5[...]
    each(G, lambda k: send(d5, k5.at[k], send_sem.at[19], grp_sem.at[12], grp=group_back(k)))

    take_all(1)
    take_all(2)

    wait_all(k5.at[pl.ds(1, G - 1)], grp_sem.at[12])
    for g in range(G):
        total[g * span:(g + 1) * span] = k5[lax.rem(g + G - me_g, G)].astype(F32)
    lcbg_ref[...] = total[:features]
    projg_ref[...] = total[features:features + HALF]
    fmg_ref[...] = total[features + HALF:features + 2 * HALF, :width]

    for h in range(3):
        wait_all(jrecv[h].at[pl.ds(1, G - 1)], grp_sem.at[6 + h])
        out = tacc[h][me_g]
        for k in range(1, G):
            out = out + jrecv[h][k].astype(F32)
        tgrad_ref[grad_parts[h], :] = out

    wait_all(r1.at[pl.ds(1, Z - 1)], send_sem.at[0])
    wait_all(feat_in.at[pl.ds(1, G - 1)], send_sem.at[1])
    wait_all(r2.at[pl.ds(1, XC - 1)], send_sem.at[2])
    wait_all(sbuf0.at[pl.ds(1, S - 1)], send_sem.at[3])
    wait_all(sbuf1.at[pl.ds(1, S - 1)], send_sem.at[4])
    wait_all(esend0.at[pl.ds(1, G - 1)], send_sem.at[5])
    wait_all(esend1.at[pl.ds(1, G - 1)], send_sem.at[6])
    for h in range(2):
        wait_all(gsend[h].at[pl.ds(1, G - 1)], send_sem.at[7 + h])
    wait_all(k1.at[pl.ds(1, G - 1)], send_sem.at[9])
    for h in range(3):
        wait_all(hsend[h].at[pl.ds(1, S - 1)], send_sem.at[10 + h])
        wait_all(jsend[h].at[pl.ds(1, G - 1)], send_sem.at[13 + h])
    wait_all(k2.at[pl.ds(1, Z - 1)], send_sem.at[16])
    wait_all(k3.at[pl.ds(1, XC - 1)], send_sem.at[17])
    wait_all(k4.at[pl.ds(1, Z - 1)], send_sem.at[18])
    wait_all(k5.at[pl.ds(1, G - 1)], send_sem.at[19])


def hand_over(*refs):
    half = len(refs) // 2
    for i in range(half):
        refs[half + i][...] = refs[i][...]


def shards(X, Z, emb_table, touched, bag_slots, feat_of_slot, lcb_weight, proj_weight, fm_weight,
           ln_gain, cotangent):
    G = lax.axis_size("grp")
    S = X * Z * 2
    XC = X * 2
    samples, slots, bags = bag_slots.shape
    table_t = emb_table.T
    width, rows = table_t.shape
    features = lcb_weight.shape[0]
    rank = proj_weight.shape[1]
    groups = X * 2
    bag_lanes = samples // 2 * LANES
    chunk = -(-(features + 2 * HALF) // (G * Z * 8)) * 8
    cut = width * 2 // 3
    heights = (cut, width - cut)
    vm = pltpu.VMEM
    dma = pltpu.SemaphoreType.DMA
    per = rows // G

    lead = width // 3
    tail = width // 6
    back_heights = (lead, width - lead)
    grad_heights = (lead, width - lead - tail, tail)
    span = (features + 2 * HALF) // G

    def two(shape_of, kind, heights=heights):
        return [vm(shape_of(height), kind) for height in heights]

    scratch = [
        vm((Z, XC, LANES), jnp.int32),
        vm((Z, XC, LANES), jnp.int32),
        vm((XC, Z, LANES), jnp.int32),
        vm((XC, Z, LANES), jnp.int32),
        vm((bags, bag_lanes), jnp.int32),
        vm((1, LANES), jnp.int32),
        vm((G, 1, LANES), jnp.int32),
        vm((groups, rows, Z * HALF), BF),
        vm((groups, Z * HALF, bag_lanes), BF),
        *two(lambda m: (S, m // 2, LANES), BF),
        *two(lambda m: (S, m // 2, LANES), BF),
        *two(lambda m: (m, Z * HALF), BF),
        *two(lambda m: (m, bag_lanes), F32),
        *two(lambda m: (G, m * 3 // 4, LANES), BF),
        *two(lambda m: (G, m * 3 // 4, LANES), BF),
        vm((2 * features, G * LANES), BF),
        *two(lambda m: (G, m * 3 // 4, LANES), BF, back_heights),
        *two(lambda m: (G, m * 3 // 4, LANES), BF, back_heights),
        vm((width, bag_lanes), BF),
        *two(lambda m: (S, m // 2, LANES), BF, grad_heights),
        *two(lambda m: (S, m // 2, LANES), BF, grad_heights),
        *two(lambda m: (G, m, per), F32, grad_heights),
        *two(lambda m: (G, m, per), BF, grad_heights),
        *two(lambda m: (G, m, per), BF, grad_heights),
        vm((G, span, features), BF),
        vm((G, span, features), BF),
        vm((Z, chunk, features), F32),
        vm((Z, chunk, features), F32),
        vm((chunk, features), F32),
        vm((XC, chunk, features), F32),
        vm((chunk, features), F32),
        vm((Z, chunk, features), F32),
        vm((span, features), BF),
        vm((G, span, features), BF),
        vm((G * span, features), F32),
        dma((20,)),
        dma((groups,)),
        dma((2 * groups,)),
        dma((3 * groups,)),
        dma((13,)),
    ]
    whole = pl.BlockSpec(memory_space=pltpu.VMEM)
    shapes = (
        jax.ShapeDtypeStruct((2, width, features), BF),
        jax.ShapeDtypeStruct((width, per), F32),
        jax.ShapeDtypeStruct((features, features), F32),
        jax.ShapeDtypeStruct((rank, features), F32),
        jax.ShapeDtypeStruct((rank, width), F32),
    )
    results = pl.pallas_call(
        functools.partial(kernel, X, Z, G),
        out_shape=shapes,
        in_specs=[whole] * 9,
        out_specs=[whole] * 5,
        scratch_shapes=scratch,
        compiler_params=pltpu.CompilerParams(
            collective_id=0, has_side_effects=True, vmem_limit_bytes=58 * 1024 * 1024
        ),
    )(
        touched.reshape(S, HALF), jnp.transpose(bag_slots, (0, 2, 1)), feat_of_slot, table_t, lcb_weight,
        proj_weight.T, fm_weight, ln_gain.reshape(1, -1), jnp.transpose(cotangent, (0, 2, 1)),
    )
    inter, tgrad, lcbg, projg, fmg = pl.pallas_call(
        hand_over,
        out_shape=shapes,
        in_specs=[whole] * 5,
        out_specs=[whole] * 5,
    )(*results)
    return (jnp.transpose(inter, (0, 2, 1)), tgrad.T, lcbg, projg.T, fmg)


def solution(mesh):
    S = mesh.shape["shard"]
    Z = mesh.shape["grp"]
    X = S // (2 * Z)
    placed = (
        P("shard", None),
        P("shard", "grp", None, None),
        P("shard", "grp", None),
        P("grp", None),
        P(),
        P(),
        P(),
        P(),
        P(("shard", "grp"), None, None),
    )
    return jax.shard_map(
        functools.partial(shards, X, Z),
        mesh=mesh,
        in_specs=placed,
        out_specs=(P(("shard", "grp"), None, None), P(("shard", "grp"), None), P(), P(), P()),
        check_vma=False,
    )
```

```python
import functools

import jax
import jax.numpy as jnp
from jax import lax
from jax.experimental import pallas as pl
from jax.experimental.pallas import tpu as pltpu
from jax.sharding import PartitionSpec as P

MESH = pl.DeviceIdType.MESH
norm_epsilon = 1e-05
LANES = 128
HALF = 64
BF = jnp.bfloat16
F32 = jnp.float32


def nn(a, b):
    return lax.dot_general(a, b, (((1,), (0,)), ((), ())), preferred_element_type=F32)


def nt(a, b):
    return lax.dot_general(a, b, (((1,), (1,)), ((), ())), preferred_element_type=F32)


def wait_all(ref, sem):
    pltpu.make_async_copy(ref, ref, sem).wait()


def pack_pair(x, low):
    m = x.shape[0] // 2
    turned = pltpu.roll(x, HALF, 1)
    even = jnp.where(low[:m], x[:m], turned[m:])
    odd = jnp.where(low[:m], turned[:m], x[m:])
    return even.astype(BF), odd.astype(BF)


def unpack_pair(even, odd, low):
    m = even.shape[0]
    even, odd = even.astype(F32), odd.astype(F32)
    top = jnp.where(low[:m], even, pltpu.roll(odd, HALF, 1))
    bottom = jnp.where(low[:m], pltpu.roll(even, HALF, 1), odd)
    return jnp.concatenate([top, bottom], axis=0).astype(BF)


def pack_dense(x, lane):
    m = x.shape[0] // 4
    last = x[3 * m:]
    tail = jnp.concatenate([pltpu.roll(last, shift, 1) for shift in (96, 64, 32)], axis=0)
    return jnp.where(lane[:3 * m] < 96, x[:3 * m], tail).astype(BF)


def unpack_dense(packed, lane):
    m = packed.shape[0] // 3
    wide = packed.astype(F32)
    first, second, third = (
        pltpu.roll(wide[i * m:(i + 1) * m], 32 * (i + 1), 1) for i in range(3)
    )
    at = lane[:m]
    last = jnp.where(at < 32, first, jnp.where(at < 64, second, third))
    return jnp.concatenate([wide, last], axis=0).astype(BF)


def kernel(
    X, Z, G,
    lists_ref, bag_ref, feat_ref, table_ref, lcb_ref, projt_ref, fm_ref, gain_ref, cot_ref,
    inter_ref, tgrad_ref, lcbg_ref, projg_ref, fmg_ref,
    l1, r1, r1t, r2, bagl, feat_own, feat_in, oh, mt,
    sbuf0, sbuf1, rbuf0, rbuf1, wide0, wide1, pooled0, pooled1, esend0, esend1, erecv0, erecv1,
    pm, gsend0, gsend1, grecv0, grecv1, gt, hsend0, hsend1, hsend2, hrecv0, hrecv1, hrecv2,
    tacc0, tacc1, tacc2, jsend0, jsend1, jsend2, jrecv0, jrecv1, jrecv2,
    w, k1, a2, k2, b3, k3, c4, k4, total,
    send_sem, list_sem, row_sem, grad_sem, grp_sem,
):
    S = X * Z * 2
    XC = X * 2
    groups = X * 2
    me_s = lax.axis_index("shard")
    me_g = lax.axis_index("grp")
    core = lax.rem(me_s, 2)
    me_z = lax.rem(lax.div(me_s, 2), Z)
    me_x = lax.div(me_s, 2 * Z)
    me_xc = me_x * 2 + core
    rows = table_ref.shape[1]
    width = table_ref.shape[0]
    features = lcb_ref.shape[0]
    samples, bags, slots = bag_ref.shape
    bag_lanes = bagl.shape[1]
    sbuf, rbuf, wide, pooled = (sbuf0, sbuf1), (rbuf0, rbuf1), (wide0, wide1), (pooled0, pooled1)
    esend, erecv = (esend0, esend1), (erecv0, erecv1)
    gsend, grecv = (gsend0, gsend1), (grecv0, grecv1)
    hsend, hrecv, tacc = (hsend0, hsend1, hsend2), (hrecv0, hrecv1, hrecv2), (tacc0, tacc1, tacc2)
    jsend, jrecv = (jsend0, jsend1, jsend2), (jrecv0, jrecv1, jrecv2)
    lead = tacc0.shape[1]
    mid = lead + tacc1.shape[1]
    back_parts = (slice(0, lead), slice(lead, width))
    grad_parts = (slice(0, lead), slice(lead, mid), slice(mid, width))
    cut = wide0.shape[0]
    parts = (slice(0, cut), slice(cut, width))

    def shard_of(x, z, c):
        return (x * Z + z) * 2 + c

    def peer(q, back):
        i = lax.rem(q, Z)
        j = lax.div(q, Z)
        dc = lax.rem(j, 2)
        dx = lax.div(j, 2)
        if back:
            x, z = lax.rem(me_x + X - dx, X), lax.rem(me_z + Z - i, Z)
        else:
            x, z = lax.rem(me_x + dx, X), lax.rem(me_z + i, Z)
        return shard_of(x, z, lax.rem(core + dc, 2))

    def z_back(k):
        return shard_of(me_x, lax.rem(me_z + Z - k, Z), core)

    def xc_back(k):
        x = lax.rem(me_x + X - lax.div(k, 2), X)
        return shard_of(x, me_z, lax.rem(core + lax.rem(k, 2), 2))

    def group_back(k):
        return lax.rem(me_g + G - k, G)

    def group_ahead(k):
        return lax.rem(me_g + k, G)

    def send(src, dst, ssem, rsem, **where):
        pltpu.make_async_remote_copy(
            src_ref=src, dst_ref=dst, send_sem=ssem, recv_sem=rsem,
            device_id=where, device_id_type=MESH,
        ).start()

    def each(count, body, first=1):
        def step(k, carry):
            body(k)
            return carry

        lax.fori_loop(first, count, step, 0)

    barrier = pltpu.get_barrier_semaphore()

    def greet(**where):
        pl.semaphore_signal(barrier, inc=1, device_id=where, device_id_type=MESH)

    each(Z, lambda k: greet(shard=z_back(k)))
    each(XC, lambda k: greet(shard=xc_back(k)))
    each(G, lambda k: greet(grp=group_back(k)))

    lists = jnp.concatenate([lists_ref[...], lists_ref[...]], axis=1)
    for z in range(Z):
        for x in range(X):
            at = (x * Z + z) * 2
            l1[z, 2 * x:2 * x + 2, :] = lists[at:at + 2]

    feat_own[...] = jnp.full(feat_own.shape, -1, jnp.int32)
    for side in range(2):
        feat_own[:, 32 * side:32 * side + 32] = feat_ref[:, :32]
        feat_own[:, 64 + 16 * side:80 + 16 * side] = feat_ref[:, 32:48]
    pl.semaphore_wait(barrier, Z - 1 + XC - 1 + G - 1)

    r1[0] = l1[me_z]

    def send_list(k):
        z = lax.rem(me_z + Z - k, Z)
        send(l1.at[z], r1.at[k], send_sem.at[0], list_sem.at[0], shard=z_back(k))

    each(Z, send_list)
    each(G, lambda k: send(feat_own, feat_in.at[k], send_sem.at[1], grp_sem.at[0], grp=group_back(k)))
    feat_in[0] = feat_own[...]
    wait_all(r1.at[pl.ds(1, Z - 1)], list_sem.at[0])
    for xc in range(XC):
        for z in range(Z):
            r1t[xc, z:z + 1, :] = r1[z, xc:xc + 1, :]

    def send_list_on(k):
        xc = lax.rem(me_x + X - lax.div(k, 2), X) * 2 + lax.rem(core + lax.rem(k, 2), 2)
        send(r1t.at[xc], r2.at[k], send_sem.at[2], list_sem.at[k], shard=xc_back(k))

    each(XC, send_list_on)
    r2[0] = r1t[me_xc]

    low1 = lax.broadcasted_iota(jnp.int32, (1, LANES), 1) < HALF
    low = lax.broadcasted_iota(jnp.int32, (cut // 2, LANES), 1) < HALF
    lane = lax.broadcasted_iota(jnp.int32, (width, LANES), 1)
    row_line = lax.broadcasted_iota(jnp.int32, (256, LANES), 0)

    def serve(j, first):
        if not first:
            wait_all(r2.at[j], list_sem.at[j])
        for p in range(Z // 2):
            want = jnp.where(low1, r2[j, 2 * p:2 * p + 1, :], r2[j, 2 * p + 1:2 * p + 2, :])
            for kb in range(rows // 256):
                hit = jnp.where(row_line == want - kb * 256, 1.0, 0.0).astype(BF)
                oh[j, kb * 256:(kb + 1) * 256, p * LANES:(p + 1) * LANES] = hit
        found = nn(table_ref[...], oh[j])
        for p in range(Z // 2):
            for h in range(2):
                even, odd = pack_pair(found[parts[h], p * LANES:(p + 1) * LANES], low)
                sbuf[h][j * Z + 2 * p] = even
                sbuf[h][j * Z + 2 * p + 1] = odd

        each(j * Z + Z, lambda q: send(sbuf0.at[q], rbuf0.at[q], send_sem.at[3], row_sem.at[j],
                                       shard=peer(q, False)),
             first=j * Z + (1 if first else 0))

    serve(0, True)
    each(groups, lambda j: serve(j, False))
    each(S, lambda q: send(sbuf1.at[q], rbuf1.at[q], send_sem.at[4], row_sem.at[groups + lax.div(q, Z)],
                           shard=peer(q, False)))
    for h in range(2):
        rbuf[h][0] = sbuf[h][0]

    bagl[...] = jnp.full(bagl.shape, -1, jnp.int32)
    for n in range(samples):
        at = n // 2 * LANES
        side = n % 2
        bagl[:, at + 32 * side:at + 32 * side + 32] = bag_ref[n, :, :32]
        bagl[:, at + 64 + 16 * side:at + 80 + 16 * side] = bag_ref[n, :, 32:48]
    slot_line = lax.broadcasted_iota(jnp.int32, (HALF, LANES), 0)

    def count(j):
        for i in range(Z):
            base = peer(j * Z + i, True) * HALF
            for c in range(bag_lanes // LANES):
                lanes = slice(c * LANES, (c + 1) * LANES)
                times = jnp.zeros((HALF, LANES), F32)
                for b in range(bags):
                    times = times + jnp.where(slot_line == bagl[b:b + 1, lanes] - base, 1.0, 0.0)
                mt[j, i * HALF:(i + 1) * HALF, lanes] = times.astype(BF)

    each(groups, count, first=0)

    wait_all(feat_in.at[pl.ds(1, G - 1)], grp_sem.at[0])
    feat_line = lax.broadcasted_iota(jnp.int32, (features, LANES), 0)
    lane1 = lax.broadcasted_iota(jnp.int32, (1, LANES), 1)
    second = ((lane1 >= 32) & (lane1 < 64)) | ((lane1 >= 80) & (lane1 < 96))
    for k in range(G):
        held = feat_line == feat_in[k]
        pm[:features, k * LANES:(k + 1) * LANES] = jnp.where(held & ~second, 1.0, 0.0).astype(BF)
        pm[features:, k * LANES:(k + 1) * LANES] = jnp.where(held & second, 1.0, 0.0).astype(BF)
    eye = jnp.where(
        lax.broadcasted_iota(jnp.int32, (width, width), 0) == lax.broadcasted_iota(jnp.int32, (width, width), 1),
        1.0, 0.0,
    )
    fm = fm_ref[...]
    fmt = nt(eye.astype(BF), fm).astype(BF)
    gain = jnp.sum(eye * gain_ref[...], axis=1, keepdims=True)

    def pool(h, j, first):
        at = j * Z
        if first:
            wait_all(rbuf[h].at[pl.ds(1, Z - 1)], row_sem.at[h * groups + j])
        else:
            wait_all(rbuf[h].at[pl.ds(at, Z)], row_sem.at[h * groups + j])
        for p in range(Z // 2):
            wide[h][:, p * LANES:(p + 1) * LANES] = unpack_pair(
                rbuf[h][at + 2 * p], rbuf[h][at + 2 * p + 1], low
            )
        now = nn(wide[h][...], mt[j])
        pooled[h][...] = now if first else pooled[h][...] + now

    for h in range(2):
        pool(h, 0, True)
        each(groups, lambda j, h=h: pool(h, j, False))
        for g in range(G):
            esend[h][group_back(g)] = pack_dense(pooled[h][:, g * LANES:(g + 1) * LANES], lane)
        each(G, lambda k, h=h: send(esend[h].at[k], erecv[h].at[k], send_sem.at[5 + h], grp_sem.at[1 + h],
                                    grp=group_back(k)))
        erecv[h][0] = esend[h][0]
    for h in range(2):
        wait_all(erecv[h].at[pl.ds(1, G - 1)], grp_sem.at[1 + h])

    arrived = jnp.concatenate([
        jnp.concatenate([unpack_dense(erecv[h][k], lane) for h in range(2)], axis=0) for k in range(G)
    ], axis=1)
    both = nt(arrived, pm[...]).astype(BF)
    lcb = lcb_ref[...]
    projt = projt_ref[...]
    grads_in = []
    later = []
    for n in range(2):
        xt = both[:, n * features:(n + 1) * features]
        low_rank = nt(xt, projt).astype(BF)
        low_rank_t = nt(projt, xt).astype(BF)
        crossed_t = nn(low_rank_t, xt).astype(BF)
        summed = xt.astype(F32) + nn(xt, lcb) + nn(fmt, crossed_t)
        center = summed - jnp.mean(summed, axis=0, keepdims=True)
        inv_std = lax.rsqrt(jnp.mean(center * center, axis=0, keepdims=True) + norm_epsilon)
        normed = center * inv_std
        inter_ref[n] = (normed * gain).astype(BF)
        scaled = cot_ref[n].astype(F32) * gain
        grad_sum = inv_std * (
            scaled
            - jnp.mean(scaled, axis=0, keepdims=True)
            - normed * jnp.mean(scaled * normed, axis=0, keepdims=True)
        )
        grad_low = grad_sum.astype(BF)
        grad_cross_t = nn(fm, grad_low).astype(BF)
        grad_proj = nt(xt, grad_cross_t).astype(BF)
        grads_in.append((
            grad_sum + nt(grad_low, lcb) + nn(low_rank, grad_cross_t) + nn(grad_proj, projt)
        ).astype(BF))
        later.append((xt, crossed_t, grad_low, grad_cross_t))

    grad_in = jnp.concatenate(grads_in, axis=1)

    def send_back(h):
        back = nn(grad_in[back_parts[h]], pm[...])
        for k in range(G):
            gsend[h][k] = pack_dense(back[:, k * LANES:(k + 1) * LANES], lane)
        each(G, lambda k: send(gsend[h].at[k], grecv[h].at[k], send_sem.at[7 + h], grp_sem.at[3 + h],
                               grp=group_ahead(k)))
        grecv[h][0] = gsend[h][0]

    send_back(0)

    lcb_grad = jnp.zeros((features, features), F32)
    proj_grad = jnp.zeros(projt.shape, F32)
    fm_grad = jnp.zeros(fm.shape, F32)
    for n in range(2):
        xt, crossed_t, grad_low, grad_cross_t = later[n]
        x = nt(pm[n * features:(n + 1) * features, :], arrived).astype(BF)
        grad_proj_t = nt(grad_cross_t, xt).astype(BF)
        fm_grad = fm_grad + nt(crossed_t, grad_low)
        proj_grad = proj_grad + nn(grad_proj_t, xt)
        lcb_grad = lcb_grad + nn(x, grad_low)
    span = w.shape[1]
    total[:features] = lcb_grad
    total[features:features + HALF] = proj_grad
    total[features + HALF:features + 2 * HALF, :] = jnp.concatenate(
        [fm_grad, jnp.zeros((fm.shape[0], total.shape[1] - width), F32)], axis=1
    ) if total.shape[1] > width else fm_grad
    for z in range(Z):
        w[z] = total[z * span:(z + 1) * span].astype(BF)
    each(Z, lambda k: send(w.at[lax.rem(me_z + Z - k, Z)], k1.at[k], send_sem.at[9], grp_sem.at[5],
                           shard=z_back(k)))
    send_back(1)

    def bring(h):
        wait_all(grecv[h].at[pl.ds(1, G - 1)], grp_sem.at[3 + h])
        for g in range(G):
            gt[back_parts[h], g * LANES:(g + 1) * LANES] = unpack_dense(grecv[h][group_back(g)], lane)

    bring(0)

    def give(h, j, first):
        slot_grad = nt(gt[grad_parts[h], :], mt[j])
        for p in range(Z // 2):
            even, odd = pack_pair(slot_grad[:, p * LANES:(p + 1) * LANES], low)
            hsend[h][j * Z + 2 * p] = even
            hsend[h][j * Z + 2 * p + 1] = odd
        if first:
            hrecv[h][0] = hsend[h][0]
        each(j * Z + Z, lambda q: send(hsend[h].at[q], hrecv[h].at[q], send_sem.at[10 + h],
                                       grad_sem.at[h * groups + j], shard=peer(q, True)),
             first=j * Z + (1 if first else 0))

    def give_some(h, first, last):
        if first == 0:
            give(h, 0, True)
            first = 1
        each(last, lambda j: give(h, j, False), first=first)

    per = rows // G

    def take(h, j, first):
        at = j * Z
        if first:
            wait_all(hrecv[h].at[pl.ds(1, Z - 1)], grad_sem.at[h * groups + j])
        else:
            wait_all(hrecv[h].at[pl.ds(at, Z)], grad_sem.at[h * groups + j])
        m = tacc[h].shape[1]
        for p in range(Z // 2):
            wide0[:m, p * LANES:(p + 1) * LANES] = unpack_pair(
                hrecv[h][at + 2 * p], hrecv[h][at + 2 * p + 1], low
            )
        for g in range(G):
            now = nt(wide0[:m, :], oh[j, g * per:(g + 1) * per, :])
            tacc[h][g] = now if first else tacc[h][g] + now

    def take_all(h):
        take(h, 0, True)
        each(groups, lambda j: take(h, j, False))

        def send_table(k):
            to = group_back(k)
            jsend[h][k] = tacc[h][to].astype(BF)
            send(jsend[h].at[k], jrecv[h].at[k], send_sem.at[13 + h], grp_sem.at[6 + h], grp=to)

        each(G, send_table)

    give_some(0, 0, groups)
    wait_all(k1.at[pl.ds(1, Z - 1)], grp_sem.at[5])
    part = w[me_z].astype(F32)
    for k in range(1, Z):
        part = part + k1[k].astype(F32)
    a2[...] = part.astype(BF)
    k2[0] = a2[...]
    each(G, lambda k: send(a2, k2.at[k], send_sem.at[16], grp_sem.at[9], grp=group_back(k)))

    bring(1)
    give_some(1, 0, groups)
    wait_all(k2.at[pl.ds(1, G - 1)], grp_sem.at[9])
    part = k2[lax.rem(G - me_g, G)].astype(F32)
    for g in range(1, G):
        part = part + k2[lax.rem(g + G - me_g, G)].astype(F32)
    b3[...] = part.astype(BF)
    k3[0] = b3[...]
    each(XC, lambda k: send(b3, k3.at[k], send_sem.at[17], grp_sem.at[10], shard=xc_back(k)))

    take_all(0)
    give_some(2, 0, groups)
    take_all(1)
    wait_all(k3.at[pl.ds(1, XC - 1)], grp_sem.at[10])

    def from_xc(s):
        dx = lax.rem(s // 2 + X - me_x, X)
        return k3[dx * 2 + lax.rem(s % 2 + core, 2)].astype(F32)

    part = from_xc(0)
    for s in range(1, XC):
        part = part + from_xc(s)
    c4[...] = part.astype(BF)
    k4[0] = c4[...]
    each(Z, lambda k: send(c4, k4.at[k], send_sem.at[18], grp_sem.at[11], shard=z_back(k)))
    take_all(2)

    wait_all(k4.at[pl.ds(1, Z - 1)], grp_sem.at[11])
    for z in range(Z):
        total[z * span:(z + 1) * span] = k4[lax.rem(z + Z - me_z, Z)].astype(F32)
    lcbg_ref[...] = total[:features]
    projg_ref[...] = total[features:features + HALF]
    fmg_ref[...] = total[features + HALF:features + 2 * HALF, :width]

    for h in range(3):
        wait_all(jrecv[h].at[pl.ds(1, G - 1)], grp_sem.at[6 + h])
        out = tacc[h][me_g]
        for k in range(1, G):
            out = out + jrecv[h][k].astype(F32)
        tgrad_ref[grad_parts[h], :] = out

    wait_all(r1.at[pl.ds(1, Z - 1)], send_sem.at[0])
    wait_all(feat_in.at[pl.ds(1, G - 1)], send_sem.at[1])
    wait_all(r2.at[pl.ds(1, XC - 1)], send_sem.at[2])
    wait_all(sbuf0.at[pl.ds(1, S - 1)], send_sem.at[3])
    wait_all(sbuf1.at[pl.ds(1, S - 1)], send_sem.at[4])
    wait_all(esend0.at[pl.ds(1, G - 1)], send_sem.at[5])
    wait_all(esend1.at[pl.ds(1, G - 1)], send_sem.at[6])
    for h in range(2):
        wait_all(gsend[h].at[pl.ds(1, G - 1)], send_sem.at[7 + h])
    wait_all(k1.at[pl.ds(1, Z - 1)], send_sem.at[9])
    for h in range(3):
        wait_all(hsend[h].at[pl.ds(1, S - 1)], send_sem.at[10 + h])
        wait_all(jsend[h].at[pl.ds(1, G - 1)], send_sem.at[13 + h])
    wait_all(k2.at[pl.ds(1, G - 1)], send_sem.at[16])
    wait_all(k3.at[pl.ds(1, XC - 1)], send_sem.at[17])
    wait_all(k4.at[pl.ds(1, Z - 1)], send_sem.at[18])


def hand_over(*refs):
    half = len(refs) // 2
    for i in range(half):
        refs[half + i][...] = refs[i][...]


def shards(X, Z, emb_table, touched, bag_slots, feat_of_slot, lcb_weight, proj_weight, fm_weight,
           ln_gain, cotangent):
    G = lax.axis_size("grp")
    S = X * Z * 2
    XC = X * 2
    samples, slots, bags = bag_slots.shape
    table_t = emb_table.T
    width, rows = table_t.shape
    features = lcb_weight.shape[0]
    rank = proj_weight.shape[1]
    groups = X * 2
    bag_lanes = samples // 2 * LANES
    cut = width * 2 // 3
    heights = (cut, width - cut)
    vm = pltpu.VMEM
    dma = pltpu.SemaphoreType.DMA
    per = rows // G

    lead = width // 3
    back_heights = (lead, width - lead)
    grad_heights = (lead, lead, width - 2 * lead)
    span = (features + 2 * HALF) // Z

    def two(shape_of, kind, heights=heights):
        return [vm(shape_of(height), kind) for height in heights]

    scratch = [
        vm((Z, XC, LANES), jnp.int32),
        vm((Z, XC, LANES), jnp.int32),
        vm((XC, Z, LANES), jnp.int32),
        vm((XC, Z, LANES), jnp.int32),
        vm((bags, bag_lanes), jnp.int32),
        vm((1, LANES), jnp.int32),
        vm((G, 1, LANES), jnp.int32),
        vm((groups, rows, Z * HALF), BF),
        vm((groups, Z * HALF, bag_lanes), BF),
        *two(lambda m: (S, m // 2, LANES), BF),
        *two(lambda m: (S, m // 2, LANES), BF),
        *two(lambda m: (m, Z * HALF), BF),
        *two(lambda m: (m, bag_lanes), F32),
        *two(lambda m: (G, m * 3 // 4, LANES), BF),
        *two(lambda m: (G, m * 3 // 4, LANES), BF),
        vm((2 * features, G * LANES), BF),
        *two(lambda m: (G, m * 3 // 4, LANES), BF, back_heights),
        *two(lambda m: (G, m * 3 // 4, LANES), BF, back_heights),
        vm((width, bag_lanes), BF),
        *two(lambda m: (S, m // 2, LANES), BF, grad_heights),
        *two(lambda m: (S, m // 2, LANES), BF, grad_heights),
        *two(lambda m: (G, m, per), F32, grad_heights),
        *two(lambda m: (G, m, per), BF, grad_heights),
        *two(lambda m: (G, m, per), BF, grad_heights),
        vm((Z, span, features), BF),
        vm((Z, span, features), BF),
        vm((span, features), BF),
        vm((G, span, features), BF),
        vm((span, features), BF),
        vm((XC, span, features), BF),
        vm((span, features), BF),
        vm((Z, span, features), BF),
        vm((Z * span, features), F32),
        dma((19,)),
        dma((groups,)),
        dma((2 * groups,)),
        dma((3 * groups,)),
        dma((12,)),
    ]
    whole = pl.BlockSpec(memory_space=pltpu.VMEM)
    shapes = (
        jax.ShapeDtypeStruct((2, width, features), BF),
        jax.ShapeDtypeStruct((width, per), F32),
        jax.ShapeDtypeStruct((features, features), F32),
        jax.ShapeDtypeStruct((rank, features), F32),
        jax.ShapeDtypeStruct((rank, width), F32),
    )
    results = pl.pallas_call(
        functools.partial(kernel, X, Z, G),
        out_shape=shapes,
        in_specs=[whole] * 9,
        out_specs=[whole] * 5,
        scratch_shapes=scratch,
        compiler_params=pltpu.CompilerParams(
            collective_id=0, has_side_effects=True, vmem_limit_bytes=58 * 1024 * 1024
        ),
    )(
        touched.reshape(S, HALF), jnp.transpose(bag_slots, (0, 2, 1)), feat_of_slot, table_t, lcb_weight,
        proj_weight.T, fm_weight, ln_gain.reshape(1, -1), jnp.transpose(cotangent, (0, 2, 1)),
    )
    inter, tgrad, lcbg, projg, fmg = pl.pallas_call(
        hand_over,
        out_shape=shapes,
        in_specs=[whole] * 5,
        out_specs=[whole] * 5,
    )(*results)
    return (jnp.transpose(inter, (0, 2, 1)), tgrad.T, lcbg, projg.T, fmg)


def solution(mesh):
    S = mesh.shape["shard"]
    Z = mesh.shape["grp"]
    X = S // (2 * Z)
    placed = (
        P("shard", None),
        P("shard", "grp", None, None),
        P("shard", "grp", None),
        P("grp", None),
        P(),
        P(),
        P(),
        P(),
        P(("shard", "grp"), None, None),
    )
    return jax.shard_map(
        functools.partial(shards, X, Z),
        mesh=mesh,
        in_specs=placed,
        out_specs=(P(("shard", "grp"), None, None), P(("shard", "grp"), None), P(), P(), P()),
        check_vma=False,
    )
```

```python
import functools

import jax
import jax.numpy as jnp
from jax import lax
from jax.experimental import pallas as pl
from jax.experimental.pallas import tpu as pltpu
from jax.sharding import PartitionSpec as P

MESH = pl.DeviceIdType.MESH
norm_epsilon = 1e-05
LANES = 128
HALF = 64
BF = jnp.bfloat16
F32 = jnp.float32


def nn(a, b):
    return lax.dot_general(a, b, (((1,), (0,)), ((), ())), preferred_element_type=F32)


def nt(a, b):
    return lax.dot_general(a, b, (((1,), (1,)), ((), ())), preferred_element_type=F32)


def wait_all(ref, sem):
    pltpu.make_async_copy(ref, ref, sem).wait()


def pack_pair(x, low):
    m = x.shape[0] // 2
    turned = pltpu.roll(x, HALF, 1)
    even = jnp.where(low[:m], x[:m], turned[m:])
    odd = jnp.where(low[:m], turned[:m], x[m:])
    return even.astype(BF), odd.astype(BF)


def unpack_pair(even, odd, low):
    m = even.shape[0]
    even, odd = even.astype(F32), odd.astype(F32)
    top = jnp.where(low[:m], even, pltpu.roll(odd, HALF, 1))
    bottom = jnp.where(low[:m], pltpu.roll(even, HALF, 1), odd)
    return jnp.concatenate([top, bottom], axis=0).astype(BF)


def pack_dense(x, lane):
    m = x.shape[0] // 4
    last = x[3 * m:]
    tail = jnp.concatenate([pltpu.roll(last, shift, 1) for shift in (96, 64, 32)], axis=0)
    return jnp.where(lane[:3 * m] < 96, x[:3 * m], tail).astype(BF)


def unpack_dense(packed, lane):
    m = packed.shape[0] // 3
    wide = packed.astype(F32)
    first, second, third = (
        pltpu.roll(wide[i * m:(i + 1) * m], 32 * (i + 1), 1) for i in range(3)
    )
    at = lane[:m]
    last = jnp.where(at < 32, first, jnp.where(at < 64, second, third))
    return jnp.concatenate([wide, last], axis=0).astype(BF)


def kernel(
    X, Z, G,
    lists_ref, bag_ref, feat_ref, table_far, lcb_far, projt_far, fm_ref, gain_ref, cot_far,
    inter_ref, tgrad_ref, lcbg_ref, projg_ref, fmg_ref,
    l1, r1, r1t, r2, bagl, feat_own, feat_in, oh, mt,
    sbuf0, sbuf1, rbuf0, rbuf1, wide0, wide1, pooled0, pooled1, esend0, esend1, erecv0, erecv1,
    pm, gsend0, gsend1, grecv0, grecv1, gt, hsend0, hsend1, hsend2, hsend3, hrecv0, hrecv1, hrecv2, hrecv3,
    tacc0, tacc1, tacc2, tacc3, jsend0, jsend1, jsend2, jsend3, jrecv0, jrecv1, jrecv2, jrecv3,
    w, k1, a2, k2, b3, k3, c4, k4, total,
    table_ref, lcb_ref, projt_ref, cot_ref,
    send_sem, list_sem, row_sem, grad_sem, grp_sem, stage_sem,
):
    S = X * Z * 2
    XC = X * 2
    groups = X * 2
    me_s = lax.axis_index("shard")
    me_g = lax.axis_index("grp")
    core = lax.rem(me_s, 2)
    me_z = lax.rem(lax.div(me_s, 2), Z)
    me_x = lax.div(me_s, 2 * Z)
    me_xc = me_x * 2 + core
    rows = table_ref.shape[1]
    width = table_ref.shape[0]
    features = lcb_ref.shape[0]
    samples, bags, slots = bag_ref.shape
    bag_lanes = bagl.shape[1]
    sbuf, rbuf, wide, pooled = (sbuf0, sbuf1), (rbuf0, rbuf1), (wide0, wide1), (pooled0, pooled1)
    esend, erecv = (esend0, esend1), (erecv0, erecv1)
    gsend, grecv = (gsend0, gsend1), (grecv0, grecv1)
    hsend, hrecv = (hsend0, hsend1, hsend2, hsend3), (hrecv0, hrecv1, hrecv2, hrecv3)
    tacc = (tacc0, tacc1, tacc2, tacc3)
    jsend, jrecv = (jsend0, jsend1, jsend2, jsend3), (jrecv0, jrecv1, jrecv2, jrecv3)
    lead = tacc0.shape[1]
    mid = lead + tacc1.shape[1]
    last = mid + tacc2.shape[1]
    back_parts = (slice(0, lead), slice(lead, width))
    grad_parts = (slice(0, lead), slice(lead, mid), slice(mid, last), slice(last, width))
    cut = wide0.shape[0]
    parts = (slice(0, cut), slice(cut, width))

    def shard_of(x, z, c):
        return (x * Z + z) * 2 + c

    def peer(q, back):
        i = lax.rem(q, Z)
        j = lax.div(q, Z)
        dc = lax.rem(j, 2)
        dx = lax.div(j, 2)
        if back:
            x, z = lax.rem(me_x + X - dx, X), lax.rem(me_z + Z - i, Z)
        else:
            x, z = lax.rem(me_x + dx, X), lax.rem(me_z + i, Z)
        return shard_of(x, z, lax.rem(core + dc, 2))

    def z_back(k):
        return shard_of(me_x, lax.rem(me_z + Z - k, Z), core)

    def xc_back(k):
        x = lax.rem(me_x + X - lax.div(k, 2), X)
        return shard_of(x, me_z, lax.rem(core + lax.rem(k, 2), 2))

    def group_back(k):
        return lax.rem(me_g + G - k, G)

    def group_ahead(k):
        return lax.rem(me_g + k, G)

    def send(src, dst, ssem, rsem, **where):
        pltpu.make_async_remote_copy(
            src_ref=src, dst_ref=dst, send_sem=ssem, recv_sem=rsem,
            device_id=where, device_id_type=MESH,
        ).start()

    def each(count, body, first=1):
        def step(k, carry):
            body(k)
            return carry

        lax.fori_loop(first, count, step, 0)

    def mixed(q):
        return lax.div(q, Z) * Z + lax.rem(lax.rem(q, Z) * 3, Z)

    def across(q, src, dst, ssem, rsem, base, back):
        at = mixed(q)
        send(src.at[at], dst.at[at], ssem, rsem.at[base + lax.div(q, Z)], shard=peer(at, back))

    barrier = pltpu.get_barrier_semaphore()

    def greet(**where):
        pl.semaphore_signal(barrier, inc=1, device_id=where, device_id_type=MESH)

    each(Z, lambda k: greet(shard=z_back(k)))
    each(XC, lambda k: greet(shard=xc_back(k)))
    each(G, lambda k: greet(grp=group_back(k)))

    staged = [
        pltpu.make_async_copy(far, near, stage_sem.at[i])
        for i, (far, near) in enumerate((
            (table_far, table_ref), (lcb_far, lcb_ref), (projt_far, projt_ref), (cot_far, cot_ref)
        ))
    ]
    for copy in staged:
        copy.start()

    lists = jnp.concatenate([lists_ref[...], lists_ref[...]], axis=1)
    for z in range(Z):
        for x in range(X):
            at = (x * Z + z) * 2
            l1[z, 2 * x:2 * x + 2, :] = lists[at:at + 2]

    feat_own[...] = jnp.full(feat_own.shape, -1, jnp.int32)
    for side in range(2):
        feat_own[:, 32 * side:32 * side + 32] = feat_ref[:, :32]
        feat_own[:, 64 + 16 * side:80 + 16 * side] = feat_ref[:, 32:48]
    pl.semaphore_wait(barrier, Z - 1 + XC - 1 + G - 1)

    r1[0] = l1[me_z]

    def send_list(k):
        z = lax.rem(me_z + Z - k, Z)
        send(l1.at[z], r1.at[k], send_sem.at[0], list_sem.at[0], shard=z_back(k))

    each(Z, send_list)
    each(G, lambda k: send(feat_own, feat_in.at[k], send_sem.at[1], grp_sem.at[0], grp=group_back(k)))
    feat_in[0] = feat_own[...]
    wait_all(r1.at[pl.ds(1, Z - 1)], list_sem.at[0])
    for xc in range(XC):
        for z in range(Z):
            r1t[xc, z:z + 1, :] = r1[z, xc:xc + 1, :]

    def send_list_on(k):
        xc = lax.rem(me_x + X - lax.div(k, 2), X) * 2 + lax.rem(core + lax.rem(k, 2), 2)
        send(r1t.at[xc], r2.at[k], send_sem.at[2], list_sem.at[k], shard=xc_back(k))

    each(XC, send_list_on)
    r2[0] = r1t[me_xc]

    low1 = lax.broadcasted_iota(jnp.int32, (1, LANES), 1) < HALF
    low = lax.broadcasted_iota(jnp.int32, (cut // 2, LANES), 1) < HALF
    lane = lax.broadcasted_iota(jnp.int32, (width, LANES), 1)
    row_line = lax.broadcasted_iota(jnp.int32, (256, LANES), 0)

    def serve(j, first):
        if not first:
            wait_all(r2.at[j], list_sem.at[j])
        for p in range(Z // 2):
            want = jnp.where(low1, r2[j, 2 * p:2 * p + 1, :], r2[j, 2 * p + 1:2 * p + 2, :])
            for kb in range(rows // 256):
                hit = jnp.where(row_line == want - kb * 256, 1.0, 0.0).astype(BF)
                oh[j, kb * 256:(kb + 1) * 256, p * LANES:(p + 1) * LANES] = hit
        found = nn(table_ref[...], oh[j])
        for p in range(Z // 2):
            for h in range(2):
                even, odd = pack_pair(found[parts[h], p * LANES:(p + 1) * LANES], low)
                sbuf[h][j * Z + 2 * p] = even
                sbuf[h][j * Z + 2 * p + 1] = odd

        each(j * Z + Z, lambda q: across(q, sbuf0, rbuf0, send_sem.at[3], row_sem, 0, False),
             first=j * Z + (1 if first else 0))

    staged[0].wait()
    serve(0, True)
    each(groups, lambda j: serve(j, False))
    each(S, lambda q: across(q, sbuf1, rbuf1, send_sem.at[4], row_sem, groups, False))
    for h in range(2):
        rbuf[h][0] = sbuf[h][0]

    for copy in staged[1:]:
        copy.wait()

    bagl[...] = jnp.full(bagl.shape, -1, jnp.int32)
    for n in range(samples):
        at = n // 2 * LANES
        side = n % 2
        bagl[:, at + 32 * side:at + 32 * side + 32] = bag_ref[n, :, :32]
        bagl[:, at + 64 + 16 * side:at + 80 + 16 * side] = bag_ref[n, :, 32:48]
    slot_line = lax.broadcasted_iota(jnp.int32, (HALF, LANES), 0)

    def count(j):
        for i in range(Z):
            base = peer(j * Z + i, True) * HALF
            for c in range(bag_lanes // LANES):
                lanes = slice(c * LANES, (c + 1) * LANES)
                times = jnp.zeros((HALF, LANES), F32)
                for b in range(bags):
                    times = times + jnp.where(slot_line == bagl[b:b + 1, lanes] - base, 1.0, 0.0)
                mt[j, i * HALF:(i + 1) * HALF, lanes] = times.astype(BF)

    each(groups, count, first=0)

    wait_all(feat_in.at[pl.ds(1, G - 1)], grp_sem.at[0])
    feat_line = lax.broadcasted_iota(jnp.int32, (features, LANES), 0)
    lane1 = lax.broadcasted_iota(jnp.int32, (1, LANES), 1)
    second = ((lane1 >= 32) & (lane1 < 64)) | ((lane1 >= 80) & (lane1 < 96))
    for k in range(G):
        held = feat_line == feat_in[k]
        pm[:features, k * LANES:(k + 1) * LANES] = jnp.where(held & ~second, 1.0, 0.0).astype(BF)
        pm[features:, k * LANES:(k + 1) * LANES] = jnp.where(held & second, 1.0, 0.0).astype(BF)
    eye = jnp.where(
        lax.broadcasted_iota(jnp.int32, (width, width), 0) == lax.broadcasted_iota(jnp.int32, (width, width), 1),
        1.0, 0.0,
    )
    fm = fm_ref[...]
    fmt = nt(eye.astype(BF), fm).astype(BF)
    gain = jnp.sum(eye * gain_ref[...], axis=1, keepdims=True)

    def pool(h, j, first):
        at = j * Z
        if first:
            wait_all(rbuf[h].at[pl.ds(1, Z - 1)], row_sem.at[h * groups + j])
        else:
            wait_all(rbuf[h].at[pl.ds(at, Z)], row_sem.at[h * groups + j])
        for p in range(Z // 2):
            wide[h][:, p * LANES:(p + 1) * LANES] = unpack_pair(
                rbuf[h][at + 2 * p], rbuf[h][at + 2 * p + 1], low
            )
        now = nn(wide[h][...], mt[j])
        pooled[h][...] = now if first else pooled[h][...] + now

    for h in range(2):
        pool(h, 0, True)
        each(groups, lambda j, h=h: pool(h, j, False))
        for g in range(G):
            esend[h][group_back(g)] = pack_dense(pooled[h][:, g * LANES:(g + 1) * LANES], lane)
        each(G, lambda k, h=h: send(esend[h].at[k], erecv[h].at[k], send_sem.at[5 + h], grp_sem.at[1 + h],
                                    grp=group_back(k)))
        erecv[h][0] = esend[h][0]
    arrived = []
    both = []
    for h in range(2):
        wait_all(erecv[h].at[pl.ds(1, G - 1)], grp_sem.at[1 + h])
        arrived.append(jnp.concatenate([unpack_dense(erecv[h][k], lane) for k in range(G)], axis=1))
        both.append(nt(arrived[h], pm[...]).astype(BF))

    arrived = jnp.concatenate(arrived, axis=0)
    both = jnp.concatenate(both, axis=0)
    lcb = lcb_ref[...]
    projt = projt_ref[...]
    grads_in = []
    later = []
    for n in range(2):
        xt = both[:, n * features:(n + 1) * features]
        low_rank = nt(xt, projt).astype(BF)
        low_rank_t = nt(projt, xt).astype(BF)
        crossed_t = nn(low_rank_t, xt).astype(BF)
        summed = xt.astype(F32) + nn(xt, lcb) + nn(fmt, crossed_t)
        center = summed - jnp.mean(summed, axis=0, keepdims=True)
        inv_std = lax.rsqrt(jnp.mean(center * center, axis=0, keepdims=True) + norm_epsilon)
        normed = center * inv_std
        inter_ref[n] = (normed * gain).astype(BF)
        scaled = cot_ref[n].astype(F32) * gain
        grad_sum = inv_std * (
            scaled
            - jnp.mean(scaled, axis=0, keepdims=True)
            - normed * jnp.mean(scaled * normed, axis=0, keepdims=True)
        )
        grad_low = grad_sum.astype(BF)
        grad_cross_t = nn(fm, grad_low).astype(BF)
        grad_proj = nt(xt, grad_cross_t).astype(BF)
        grads_in.append((
            grad_sum + nt(grad_low, lcb) + nn(low_rank, grad_cross_t) + nn(grad_proj, projt)
        ).astype(BF))
        later.append((xt, crossed_t, grad_low, grad_cross_t))

    grad_in = jnp.concatenate(grads_in, axis=1)

    def send_back(h):
        back = nn(grad_in[back_parts[h]], pm[...])
        for k in range(G):
            gsend[h][k] = pack_dense(back[:, k * LANES:(k + 1) * LANES], lane)
        each(G, lambda k: send(gsend[h].at[k], grecv[h].at[k], send_sem.at[7 + h], grp_sem.at[3 + h],
                               grp=group_ahead(k)))
        grecv[h][0] = gsend[h][0]

    send_back(0)

    lcb_grad = jnp.zeros((features, features), F32)
    proj_grad = jnp.zeros(projt.shape, F32)
    fm_grad = jnp.zeros(fm.shape, F32)
    for n in range(2):
        xt, crossed_t, grad_low, grad_cross_t = later[n]
        x = nt(pm[n * features:(n + 1) * features, :], arrived).astype(BF)
        grad_proj_t = nt(grad_cross_t, xt).astype(BF)
        fm_grad = fm_grad + nt(crossed_t, grad_low)
        proj_grad = proj_grad + nn(grad_proj_t, xt)
        lcb_grad = lcb_grad + nn(x, grad_low)
    span = w.shape[1]
    total[:features] = lcb_grad
    total[features:features + HALF] = proj_grad
    total[features + HALF:features + 2 * HALF, :] = jnp.concatenate(
        [fm_grad, jnp.zeros((fm.shape[0], total.shape[1] - width), F32)], axis=1
    ) if total.shape[1] > width else fm_grad
    for z in range(Z):
        w[z] = total[z * span:(z + 1) * span].astype(BF)
    each(Z, lambda k: send(w.at[lax.rem(me_z + Z - k, Z)], k1.at[k], send_sem.at[9], grp_sem.at[5],
                           shard=z_back(k)))
    send_back(1)

    def bring(h):
        wait_all(grecv[h].at[pl.ds(1, G - 1)], grp_sem.at[3 + h])
        for g in range(G):
            gt[back_parts[h], g * LANES:(g + 1) * LANES] = unpack_dense(grecv[h][group_back(g)], lane)

    bring(0)

    def give(h, j, first):
        made = (0,) if h == 0 else (1, 2, 3)
        low_row, high_row = grad_parts[made[0]].start, grad_parts[made[-1]].stop
        slot_grad = nt(gt[low_row:high_row, :], mt[j])
        for to in made:
            part = slot_grad[grad_parts[to].start - low_row:grad_parts[to].stop - low_row]
            for p in range(Z // 2):
                even, odd = pack_pair(part[:, p * LANES:(p + 1) * LANES], low)
                hsend[to][j * Z + 2 * p] = even
                hsend[to][j * Z + 2 * p + 1] = odd
            if first:
                hrecv[to][0] = hsend[to][0]
        each(j * Z + Z, lambda q: across(q, hsend[h], hrecv[h], send_sem.at[10 + h], grad_sem, h * groups, True),
             first=j * Z + (1 if first else 0))

    def give_some(h, first, last):
        if first == 0:
            give(h, 0, True)
            first = 1
        each(last, lambda j: give(h, j, False), first=first)

    per = rows // G

    def take(h, j, first):
        at = j * Z
        if first:
            wait_all(hrecv[h].at[pl.ds(1, Z - 1)], grad_sem.at[h * groups + j])
        else:
            wait_all(hrecv[h].at[pl.ds(at, Z)], grad_sem.at[h * groups + j])
        m = tacc[h].shape[1]
        for p in range(Z // 2):
            wide0[:m, p * LANES:(p + 1) * LANES] = unpack_pair(
                hrecv[h][at + 2 * p], hrecv[h][at + 2 * p + 1], low
            )
        for g in range(G):
            now = nt(wide0[:m, :], oh[j, g * per:(g + 1) * per, :])
            tacc[h][g] = now if first else tacc[h][g] + now

    def take_all(h):
        take(h, 0, True)
        each(groups, lambda j: take(h, j, False))

        def send_table(k):
            to = group_back(k)
            jsend[h][k] = tacc[h][to].astype(BF)
            send(jsend[h].at[k], jrecv[h].at[k], send_sem.at[14 + h], grp_sem.at[6 + h], grp=to)

        each(G, send_table)

    give_some(0, 0, groups)
    wait_all(k1.at[pl.ds(1, Z - 1)], grp_sem.at[5])
    part = w[me_z].astype(F32)
    for k in range(1, Z):
        part = part + k1[k].astype(F32)
    a2[...] = part.astype(BF)
    k2[0] = a2[...]
    each(G, lambda k: send(a2, k2.at[k], send_sem.at[18], grp_sem.at[10], grp=group_back(k)))

    bring(1)
    give_some(1, 0, groups)
    wait_all(k2.at[pl.ds(1, G - 1)], grp_sem.at[10])
    part = k2[lax.rem(G - me_g, G)].astype(F32)
    for g in range(1, G):
        part = part + k2[lax.rem(g + G - me_g, G)].astype(F32)
    b3[...] = part.astype(BF)
    k3[0] = b3[...]
    each(XC, lambda k: send(b3, k3.at[k], send_sem.at[19], grp_sem.at[11], shard=xc_back(k)))

    for h in (2, 3):
        each(S, lambda q, h=h: across(q, hsend[h], hrecv[h], send_sem.at[10 + h], grad_sem, h * groups, True))

    take_all(0)
    take_all(1)
    wait_all(k3.at[pl.ds(1, XC - 1)], grp_sem.at[11])

    def from_xc(s):
        dx = lax.rem(s // 2 + X - me_x, X)
        return k3[dx * 2 + lax.rem(s % 2 + core, 2)].astype(F32)

    part = from_xc(0)
    for s in range(1, XC):
        part = part + from_xc(s)
    c4[...] = part.astype(BF)
    k4[0] = c4[...]
    each(Z, lambda k: send(c4, k4.at[k], send_sem.at[20], grp_sem.at[12], shard=z_back(k)))
    take_all(2)
    take_all(3)

    wait_all(k4.at[pl.ds(1, Z - 1)], grp_sem.at[12])
    for z in range(Z):
        total[z * span:(z + 1) * span] = k4[lax.rem(z + Z - me_z, Z)].astype(F32)
    lcbg_ref[...] = total[:features]
    projg_ref[...] = total[features:features + HALF]
    fmg_ref[...] = total[features + HALF:features + 2 * HALF, :width]

    for h in range(4):
        wait_all(jrecv[h].at[pl.ds(1, G - 1)], grp_sem.at[6 + h])
        out = tacc[h][me_g]
        for k in range(1, G):
            out = out + jrecv[h][k].astype(F32)
        tgrad_ref[grad_parts[h], :] = out

    wait_all(r1.at[pl.ds(1, Z - 1)], send_sem.at[0])
    wait_all(feat_in.at[pl.ds(1, G - 1)], send_sem.at[1])
    wait_all(r2.at[pl.ds(1, XC - 1)], send_sem.at[2])
    wait_all(sbuf0.at[pl.ds(1, S - 1)], send_sem.at[3])
    wait_all(sbuf1.at[pl.ds(1, S - 1)], send_sem.at[4])
    wait_all(esend0.at[pl.ds(1, G - 1)], send_sem.at[5])
    wait_all(esend1.at[pl.ds(1, G - 1)], send_sem.at[6])
    for h in range(2):
        wait_all(gsend[h].at[pl.ds(1, G - 1)], send_sem.at[7 + h])
    wait_all(k1.at[pl.ds(1, Z - 1)], send_sem.at[9])
    for h in range(4):
        wait_all(hsend[h].at[pl.ds(1, S - 1)], send_sem.at[10 + h])
        wait_all(jsend[h].at[pl.ds(1, G - 1)], send_sem.at[14 + h])
    wait_all(k2.at[pl.ds(1, G - 1)], send_sem.at[18])
    wait_all(k3.at[pl.ds(1, XC - 1)], send_sem.at[19])
    wait_all(k4.at[pl.ds(1, Z - 1)], send_sem.at[20])


def hand_over(*refs):
    half = len(refs) // 2
    sems = refs[-1]
    copies = [pltpu.make_async_copy(refs[i], refs[half + i], sems.at[i]) for i in range(half)]
    for copy in copies:
        copy.start()
    for copy in copies:
        copy.wait()


def shards(X, Z, emb_table, touched, bag_slots, feat_of_slot, lcb_weight, proj_weight, fm_weight,
           ln_gain, cotangent):
    G = lax.axis_size("grp")
    S = X * Z * 2
    XC = X * 2
    samples, slots, bags = bag_slots.shape
    table_t = emb_table.T
    width, rows = table_t.shape
    features = lcb_weight.shape[0]
    rank = proj_weight.shape[1]
    groups = X * 2
    bag_lanes = samples // 2 * LANES
    cut = width * 2 // 3
    heights = (cut, width - cut)
    vm = pltpu.VMEM
    dma = pltpu.SemaphoreType.DMA
    per = rows // G

    lead = width // 3
    back_heights = (lead, width - lead)
    tail = lead // 2
    grad_heights = (lead, lead, tail, width - 2 * lead - tail)
    span = (features + 2 * HALF) // Z

    def two(shape_of, kind, heights=heights):
        return [vm(shape_of(height), kind) for height in heights]

    scratch = [
        vm((Z, XC, LANES), jnp.int32),
        vm((Z, XC, LANES), jnp.int32),
        vm((XC, Z, LANES), jnp.int32),
        vm((XC, Z, LANES), jnp.int32),
        vm((bags, bag_lanes), jnp.int32),
        vm((1, LANES), jnp.int32),
        vm((G, 1, LANES), jnp.int32),
        vm((groups, rows, Z * HALF), BF),
        vm((groups, Z * HALF, bag_lanes), BF),
        *two(lambda m: (S, m // 2, LANES), BF),
        *two(lambda m: (S, m // 2, LANES), BF),
        *two(lambda m: (m, Z * HALF), BF),
        *two(lambda m: (m, bag_lanes), F32),
        *two(lambda m: (G, m * 3 // 4, LANES), BF),
        *two(lambda m: (G, m * 3 // 4, LANES), BF),
        vm((2 * features, G * LANES), BF),
        *two(lambda m: (G, m * 3 // 4, LANES), BF, back_heights),
        *two(lambda m: (G, m * 3 // 4, LANES), BF, back_heights),
        vm((width, bag_lanes), BF),
        *two(lambda m: (S, m // 2, LANES), BF, grad_heights),
        *two(lambda m: (S, m // 2, LANES), BF, grad_heights),
        *two(lambda m: (G, m, per), F32, grad_heights),
        *two(lambda m: (G, m, per), BF, grad_heights),
        *two(lambda m: (G, m, per), BF, grad_heights),
        vm((Z, span, features), BF),
        vm((Z, span, features), BF),
        vm((span, features), BF),
        vm((G, span, features), BF),
        vm((span, features), BF),
        vm((XC, span, features), BF),
        vm((span, features), BF),
        vm((Z, span, features), BF),
        vm((Z * span, features), F32),
        vm(table_t.shape, BF),
        vm(lcb_weight.shape, BF),
        vm((rank, features), BF),
        vm((2, width, features), BF),
        dma((21,)),
        dma((groups,)),
        dma((2 * groups,)),
        dma((4 * groups,)),
        dma((13,)),
        dma((4,)),
    ]
    whole = pl.BlockSpec(memory_space=pltpu.VMEM)
    far = pl.BlockSpec(memory_space=pl.ANY)
    shapes = (
        jax.ShapeDtypeStruct((2, width, features), BF),
        jax.ShapeDtypeStruct((width, per), F32),
        jax.ShapeDtypeStruct((features, features), F32),
        jax.ShapeDtypeStruct((rank, features), F32),
        jax.ShapeDtypeStruct((rank, width), F32),
    )
    results = pl.pallas_call(
        functools.partial(kernel, X, Z, G),
        out_shape=shapes,
        in_specs=[whole, whole, whole, far, far, far, whole, whole, far],
        out_specs=[whole] * 5,
        scratch_shapes=scratch,
        compiler_params=pltpu.CompilerParams(
            collective_id=0, has_side_effects=True, vmem_limit_bytes=58 * 1024 * 1024
        ),
    )(
        touched.reshape(S, HALF), jnp.transpose(bag_slots, (0, 2, 1)), feat_of_slot, table_t, lcb_weight,
        proj_weight.T, fm_weight, ln_gain.reshape(1, -1), jnp.transpose(cotangent, (0, 2, 1)),
    )
    inter, tgrad, lcbg, projg, fmg = pl.pallas_call(
        hand_over,
        out_shape=shapes,
        in_specs=[far] * 5,
        out_specs=[whole] * 5,
        scratch_shapes=[dma((5,))],
    )(*results)
    return (jnp.transpose(inter, (0, 2, 1)), tgrad.T, lcbg, projg.T, fmg)


def solution(mesh):
    S = mesh.shape["shard"]
    Z = mesh.shape["grp"]
    X = S // (2 * Z)
    placed = (
        P("shard", None),
        P("shard", "grp", None, None),
        P("shard", "grp", None),
        P("grp", None),
        P(),
        P(),
        P(),
        P(),
        P(("shard", "grp"), None, None),
    )
    return jax.shard_map(
        functools.partial(shards, X, Z),
        mesh=mesh,
        in_specs=placed,
        out_specs=(P(("shard", "grp"), None, None), P(("shard", "grp"), None), P(), P(), P()),
        check_vma=False,
    )
```
